32 devices in a mesh: dir: 4 (over x, core), elem: 8 (over z, y).
Axes of the slice: x: 2, y: 2, z: 4, core: 2. Of those that a mesh axis runs over, the one named last changes fastest.
Arguments:
- panel_angles: float32 [2, 16384], P(None, 'elem'), may hold values from -3.140625 to 3.140625
- impedance: float32 [16384], P('elem'), may hold values from 0.3 to 3
- quad_count: int32 [16384], P('elem'), may hold values from 1 to 4
- receivers: int32 [1024], replicated, may hold values from 0 to 4095
- farfield_data: float32 [2, 64, 1024], P(None, 'dir'), may hold values from -24 to 24
- warm_density: float32 [2, 64, 16384], P(None, 'dir', 'elem'), may hold values from -6 to 6
Outputs:
- gradient: float32 [16384], P('elem')
- density: float32 [2, 64, 16384], P(None, 'dir', 'elem')
The draws below stay inside these ranges and needn't reach their ends.
Inputs may be any that keep to these rules, and one draw needn't show every extreme that they name: Index into a lattice of 4096 directions; receivers may share an index.
All inputs are finite; a program needn't handle non-finite values.
Results may differ from the reference program's by a relative error of at most 0.0038.
Values may be sent and summed in bfloat16 or wider, within the bound.
A program may use at most 256 MiB of HBM per device.

```python
import math
import jax
import jax.numpy as jnp
from jax import lax

PANELS = 16384
RECV = 1024
ITERS = 1
RBANK = 4096
NDIR = 64


def draw_farfield_data(key, part):
    keys = jax.random.split(jax.random.fold_in(key, 7177), 1)
    values = 3.0 * jax.random.normal(keys[0], (2, NDIR, RECV), jnp.float32)
    return jnp.clip(values, -24.0, 24.0)


def touch_ends(entries, own_key, low, top_value):
    index_at = [jax.random.randint(jax.random.fold_in(own_key, axis), (), 0, length) for axis, length in enumerate(entries.shape)]
    widest = entries.shape.index(max(entries.shape))
    next_to = index_at[:widest] + [(index_at[widest] + 1) % entries.shape[widest]] + index_at[widest + 1:]
    return entries.at[tuple(index_at)].set(low).at[tuple(next_to)].set(top_value)


def level_of(rng, shape, pieces, least, largest):
    factor_of = 1.0
    for dim, blocks in pieces:
        draws = jax.random.uniform(jax.random.fold_in(jax.random.fold_in(rng, 6), dim), (blocks,), jnp.float32, least / len(pieces), largest / len(pieces))
        factor_of = factor_of * jnp.repeat(jnp.exp(draws), shape[dim] // blocks).reshape((-1,) + (1,) * (len(shape) - 1 - dim))
    return factor_of


def bell_draw(key, extent, scale, most, cuts=(), held_as=jnp.bfloat16):
    factor_of = level_of(key, extent, cuts, -0.22, 0.18) if cuts else 1.0
    drawn = jax.random.normal(key, extent, jnp.float32) * scale * factor_of
    return jnp.minimum(jnp.maximum(drawn, -most), most).astype(held_as)


def setup_inputs(seed: int = 0) -> dict:
    arg_keys = jax.random.split(jax.random.key(seed), 7)
    return {
        "panel_angles": jnp.clip(jax.random.uniform(arg_keys[0], (2, PANELS), jnp.float32, -3.140625, 3.140625), -3.140625, 3.140625),
        "impedance": jnp.clip(jnp.exp(math.log(3.0) - 2.3025851 * jax.random.uniform(arg_keys[1], (PANELS,), jnp.float32) ** level_of(arg_keys[1], (PANELS,), ((0, 8),), -0.2, 0.2)), 0.3, 3.0),
        "quad_count": touch_ends(jax.random.randint(arg_keys[2], (PANELS,), 1, 5), jax.random.fold_in(arg_keys[2], 1), 1, 4).astype(jnp.int32),
        "receivers": touch_ends(jax.random.randint(arg_keys[3], (RECV,), 0, RBANK), jax.random.fold_in(arg_keys[3], 1), 0, RBANK - 1).astype(jnp.int32),
        "farfield_data": draw_farfield_data(jax.random.fold_in(arg_keys[6], 71), 0),
        "warm_density": bell_draw(arg_keys[5], (2, NDIR, PANELS), 1.0, 6.0, ((1, 4), (2, 8)), jnp.float32),
    }


WAVENUM = 32.0
SOFTEN = 0.0025
tile_rows = 512

def positions(angles):
    phi = angles[0]
    psi = angles[1]
    return jnp.stack([4.0 * jnp.cos(psi), jnp.sin(psi) * jnp.cos(phi), 0.6 * jnp.sin(psi) * jnp.sin(phi)])

def weights(counts):
    return counts.astype(jnp.float32) * (0.5 / (4.0 * math.sqrt(PANELS)))

def lattice(index, count):
    where = index.astype(jnp.float32)
    height = 1.0 - (2.0 * where + 1.0) / count
    radius = jnp.sqrt(1.0 - height * height)
    turn = where * (math.pi * (3.0 - math.sqrt(5.0)))
    return jnp.stack([radius * jnp.cos(turn), radius * jnp.sin(turn), height])

def plane(dvec, pos):
    phase = WAVENUM * lax.optimization_barrier(jnp.sum(dvec[:, :, None] * pos[:, None, :], axis=0))
    return jnp.stack([jnp.cos(phase), jnp.sin(phase)])

def far_table(pos, rdir):
    theta = WAVENUM * lax.optimization_barrier(jnp.sum(pos[:, :, None] * rdir[:, None, :], axis=0))
    return (jnp.cos(theta).astype(jnp.bfloat16), jnp.sin(theta).astype(jnp.bfloat16))

def kernel_tile(src, tgt):
    dist = lax.optimization_barrier(jnp.sum((src[:, :, None] - tgt[:, None, :]) ** 2, axis=0))
    rho = jnp.sqrt(dist + SOFTEN)
    return ((jnp.cos(WAVENUM * rho) / rho).astype(jnp.bfloat16), (jnp.sin(WAVENUM * rho) / rho).astype(jnp.bfloat16))

def apply(vec, cos_t, sin_t, sign, axis):
    half = vec.shape[1]
    stacked = vec.reshape(2 * half, vec.shape[2])
    dims = (((1,), (axis,)), ((), ()))
    first = lax.dot_general(stacked, cos_t, dims, preferred_element_type=jnp.float32)
    second = lax.dot_general(stacked, sin_t, dims, preferred_element_type=jnp.float32)
    real = first[:half] - sign * second[half:]
    imag = first[half:] + sign * second[:half]
    return jnp.stack([real, imag])

def full_apply(vec, pos, sign):
    block = min(tile_rows, PANELS)
    count = PANELS // block
    targets = jnp.transpose(pos.reshape(3, count, block), (1, 0, 2))

    def one(tgt):
        cos_t, sin_t = kernel_tile(pos, tgt)
        return apply(vec, cos_t, sin_t, sign, 0)
    out = lax.map(one, targets)
    return jnp.transpose(out, (1, 2, 0, 3)).reshape(2, vec.shape[1], PANELS)

def reference(panel_angles, impedance, quad_count, receivers, farfield_data, warm_density):
    pos = positions(panel_angles)
    wgt = weights(quad_count)
    wz = wgt * impedance
    ndir = farfield_data.shape[1]
    dvec = lattice(jnp.arange(ndir, dtype=jnp.int32), ndir)
    incident = plane(dvec, pos)
    sigmas = [warm_density]
    state = warm_density
    for step in range(ITERS):
        moved = (wz * state).astype(jnp.bfloat16)
        state = incident - full_apply(moved, pos, 1.0)
        sigmas.append(state)
    rdir = lattice(receivers, RBANK)
    cos_t, sin_t = far_table(pos, rdir)
    farfield = apply((wgt * state).astype(jnp.bfloat16), cos_t, sin_t, -1.0, 0)
    misfit = (farfield - farfield_data).astype(jnp.bfloat16)
    adjoint = wgt * apply(misfit, cos_t, sin_t, 1.0, 1)
    total = jnp.zeros((PANELS,), jnp.float32)
    for step in reversed(range(ITERS)):
        back = -full_apply(adjoint.astype(jnp.bfloat16), pos, -1.0)
        total = total + lax.optimization_barrier(jnp.sum(back * sigmas[step], axis=(0, 1)))
        adjoint = wz * back
    return (total / ndir, state)
```

```python
import math

import jax
import jax.numpy as jnp
from jax import lax
from jax.experimental import pallas as pl
from jax.experimental.pallas import tpu as pltpu
from jax.sharding import PartitionSpec as P

PANELS = 16384
RBANK = 4096

WAVENUM = 32.0
SOFTEN = 0.0025
TURNS = WAVENUM / (2.0 * math.pi)
MAGIC = 12582912.0

COS = (0.99999921, -19.73898036, 64.92865742, -85.27162153, 58.79049212, -21.07110563)
SIN = (6.28316113, -41.33683183, 81.44770647, -74.9094197, 33.54835515)

f32 = jnp.float32
bf16 = jnp.bfloat16


def positions(angles):
    phi = angles[0]
    psi = angles[1]
    return jnp.stack(
        [4.0 * jnp.cos(psi), jnp.sin(psi) * jnp.cos(phi), 0.6 * jnp.sin(psi) * jnp.sin(phi)]
    )


def weights(counts):
    return counts.astype(f32) * (0.5 / (4.0 * math.sqrt(PANELS)))


def lattice(index, count):
    where = index.astype(f32)
    height = 1.0 - (2.0 * where + 1.0) / count
    radius = jnp.sqrt(1.0 - height * height)
    turn = where * (math.pi * (3.0 - math.sqrt(5.0)))
    return jnp.stack([radius * jnp.cos(turn), radius * jnp.sin(turn), height])


def plane(dvec, pos):
    phase = WAVENUM * jnp.sum(dvec[:, :, None] * pos[:, None, :], axis=0)
    return jnp.stack([jnp.cos(phase), jnp.sin(phase)])


def pieces(x):
    hi = lax.reduce_precision(x, 8, 7)
    mid = lax.reduce_precision(x - hi, 8, 7)
    return hi, mid, (x - hi) - mid


def product_rows(a, b):
    ah, am, al = pieces(a)
    bh, bm, bl = pieces(b)
    left = jnp.concatenate([ah, ah, am, am, ah, al], axis=0)
    right = jnp.concatenate([bh, bm, bh, bm, bl, bh], axis=0)
    return left, right


def pad_rows(x):
    return jnp.pad(x, ((0, 32 - x.shape[0]), (0, 0))).astype(bf16)


def distance_rows(src, tgt):
    left, right = product_rows(-2.0 * src, tgt)
    ones_s = jnp.ones((3, src.shape[1]), f32)
    ones_t = jnp.ones((3, tgt.shape[1]), f32)
    sq_s = jnp.stack(pieces(jnp.sum(src * src, axis=0)))
    sq_t = jnp.stack(pieces(jnp.sum(tgt * tgt, axis=0) + SOFTEN * TURNS * TURNS))
    left = jnp.concatenate([left, sq_s, ones_s], axis=0)
    right = jnp.concatenate([right, ones_t, sq_t], axis=0)
    return pad_rows(left), pad_rows(right)


def horner(coefs, z, scale):
    total = coefs[-1] * scale
    for c in coefs[-2::-1]:
        total = total * z + c * scale
    return total


def green(d2):
    inv = lax.rsqrt(d2)
    t = d2 * inv
    r = t - ((t + MAGIC) - MAGIC)
    z = r * r
    cos_k = horner(COS, z, TURNS) * inv
    sin_k = horner(SIN, z, TURNS) * (r * inv)
    return cos_k.astype(bf16), sin_k.astype(bf16)


def mm(a, b):
    return lax.dot_general(a, b, (((1,), (0,)), ((), ())), preferred_element_type=f32)


def mt(a, b):
    return lax.dot_general(a, b, (((1,), (1,)), ((), ())), preferred_element_type=f32)


def chunk_of(total, most):
    size = min(total, most)
    while total % size:
        size //= 2
    return size


def forward_body(sb, a_ref, b_ref, va_ref, vb_ref, c_ref, s_ref, u_ref):
    count = a_ref.shape[0] // sb

    def make(k):
        rows = pl.ds(pl.multiple_of(k * sb, sb), sb)
        cos_k, sin_k = green(mm(a_ref[rows, :], b_ref[...]))
        c_ref[rows, :] = cos_k
        s_ref[rows, :] = sin_k

    def use(k):
        rows = pl.ds(pl.multiple_of(k * sb, sb), sb)
        return mm(va_ref[:, rows], c_ref[rows, :]) + mm(vb_ref[:, rows], s_ref[rows, :])

    u_ref[...] = jnp.zeros_like(u_ref)
    make(0)

    def body(k, carry):
        u_ref[...] += use(k - 1)
        make(k)
        return carry

    lax.fori_loop(1, count, body, 0)
    u_ref[...] += use(count - 1)


def forward(a, b, va, vb):
    sources = a.shape[0]
    targets = b.shape[1]
    lanes = va.shape[0]
    tb = chunk_of(targets, 256)
    sb = chunk_of(sources, 256)
    whole = lambda x: pl.BlockSpec(x.shape, lambda i: (0, 0))
    col = lambda n: pl.BlockSpec((n, tb), lambda i: (0, i))
    cells = sources * targets
    return pl.pallas_call(
        lambda *refs: forward_body(sb, *refs),
        grid=(targets // tb,),
        in_specs=[whole(a), col(32), whole(va), whole(vb)],
        out_specs=[col(sources), col(sources), col(lanes)],
        out_shape=[
            jax.ShapeDtypeStruct((sources, targets), bf16),
            jax.ShapeDtypeStruct((sources, targets), bf16),
            jax.ShapeDtypeStruct((lanes, targets), f32),
        ],
        compiler_params=pltpu.CompilerParams(vmem_limit_bytes=48 * 2**20),
        cost_estimate=pl.CostEstimate(
            flops=cells * (30 + 4 * lanes), bytes_accessed=4 * cells, transcendentals=cells
        ),
        name="forward",
    )(a, b, va, vb)


def backward_body(ma_ref, mb_ref, c_ref, s_ref, v_ref, g_ref):
    nu = mt(ma_ref[...], c_ref[...]) + mt(mb_ref[...], s_ref[...])
    g_ref[...] = jnp.sum(nu * v_ref[...].astype(f32), axis=0, keepdims=True)


def backward(ma, mb, cos_k, sin_k, v):
    sources, targets = cos_k.shape
    lanes = ma.shape[0]
    sb = chunk_of(sources, 256)
    whole = lambda x: pl.BlockSpec(x.shape, lambda i: (0, 0))
    row = pl.BlockSpec((sb, targets), lambda i: (i, 0))
    col = lambda n: pl.BlockSpec((n, sb), lambda i: (0, i))
    cells = sources * targets
    return pl.pallas_call(
        backward_body,
        grid=(sources // sb,),
        in_specs=[whole(ma), whole(mb), row, row, col(lanes)],
        out_specs=col(1),
        out_shape=jax.ShapeDtypeStruct((1, sources), f32),
        compiler_params=pltpu.CompilerParams(vmem_limit_bytes=48 * 2**20),
        cost_estimate=pl.CostEstimate(
            flops=cells * 4 * lanes, bytes_accessed=4 * cells, transcendentals=0
        ),
        name="backward",
    )(ma, mb, cos_k, sin_k, v)


def table_body(rb, a_ref, b_ref, c_ref, s_ref):
    def body(k, carry):
        rows = pl.ds(pl.multiple_of(k * rb, rb), rb)
        t = mm(a_ref[rows, :], b_ref[...])
        r = t - ((t + MAGIC) - MAGIC)
        z = r * r
        c_ref[rows, :] = horner(COS, z, 1.0).astype(bf16)
        s_ref[rows, :] = (horner(SIN, z, 1.0) * r).astype(bf16)
        return carry

    lax.fori_loop(0, a_ref.shape[0] // rb, body, 0)


def far_table(a, b):
    rows = a.shape[0]
    recv = b.shape[1]
    tb = chunk_of(recv, 256)
    rb = chunk_of(rows, 256)
    col = lambda n: pl.BlockSpec((n, tb), lambda i: (0, i))
    out = jax.ShapeDtypeStruct((rows, recv), bf16)
    cells = rows * recv
    return pl.pallas_call(
        lambda *refs: table_body(rb, *refs),
        grid=(recv // tb,),
        in_specs=[pl.BlockSpec(a.shape, lambda i: (0, 0)), col(32)],
        out_specs=[col(rows), col(rows)],
        out_shape=[out, out],
        compiler_params=pltpu.CompilerParams(vmem_limit_bytes=48 * 2**20),
        cost_estimate=pl.CostEstimate(flops=cells * 30, bytes_accessed=4 * cells, transcendentals=0),
        name="far_table",
    )(a, b)


def apply(vec, cos_t, sin_t, sign, axis):
    half = vec.shape[1]
    stacked = vec.reshape(2 * half, vec.shape[2])
    dims = (((1,), (axis,)), ((), ()))
    first = lax.dot_general(stacked, cos_t, dims, preferred_element_type=f32)
    second = lax.dot_general(stacked, sin_t, dims, preferred_element_type=f32)
    real = first[:half] - sign * second[half:]
    imag = first[half:] + sign * second[:half]
    return jnp.stack([real, imag])


def on_device(panel_angles, impedance, quad_count, receivers, farfield_data, warm_density):
    rows = impedance.shape[0]
    count_dir = farfield_data.shape[1]
    groups = lax.axis_size("dir")
    blocks = lax.axis_size("elem")
    ndir = count_dir * groups
    sub = rows // groups
    lanes = 2 * ndir
    me = lax.axis_index("dir")

    w_loc = weights(quad_count)
    wz_loc = w_loc * impedance
    pos_loc = positions(panel_angles)
    turn_loc = pos_loc * TURNS

    src = lax.dynamic_slice_in_dim(turn_loc, me * sub, sub, 1)
    src = lax.all_gather(src, "elem", axis=1, tiled=True)
    v = (wz_loc * warm_density).astype(bf16)
    v = v.reshape(2, count_dir, groups, sub)
    v = lax.all_to_all(v, "dir", 2, 0, tiled=False)
    v = lax.all_gather(v, "elem", axis=0)
    v = jnp.transpose(v, (1, 2, 3, 0, 4)).reshape(groups, 2, count_dir, blocks * sub)
    va = v.reshape(lanes, blocks * sub)
    vb = jnp.stack([-v[:, 1], v[:, 0]], axis=1).reshape(lanes, blocks * sub)

    left, right = distance_rows(src, turn_loc)
    cos_k, sin_k, image = forward(left.T, right, va, vb)
    image = lax.psum_scatter(
        image.reshape(groups, 2, count_dir, rows), "dir", scatter_dimension=0, tiled=False
    )

    dvec = lattice(me * count_dir + jnp.arange(count_dir, dtype=jnp.int32), ndir)
    state = plane(dvec, pos_loc) - image

    left, right = product_rows(turn_loc, lattice(receivers, RBANK))
    cos_t, sin_t = far_table(pad_rows(left).T, pad_rows(right))
    partial_far = apply((w_loc * state).astype(bf16), cos_t, sin_t, -1.0, 0)
    farfield = lax.psum(partial_far, "elem")
    misfit = (farfield - farfield_data).astype(bf16)
    adjoint = (w_loc * apply(misfit, cos_t, sin_t, 1.0, 1)).astype(bf16)

    mu = lax.all_gather(adjoint, "dir", axis=0)
    ma = mu.reshape(lanes, rows)
    mb = jnp.stack([mu[:, 1], -mu[:, 0]], axis=1).reshape(lanes, rows)
    grad = backward(ma, mb, cos_k, sin_k, va)
    grad = lax.psum_scatter(grad.reshape(blocks, sub), "elem", scatter_dimension=0, tiled=False)
    grad = lax.all_gather(grad, "dir", axis=0, tiled=True)
    return (grad / (-ndir * wz_loc), state)


def solution(mesh):
    placed = (
        P(None, "elem"),
        P("elem"),
        P("elem"),
        P(),
        P(None, "dir", None),
        P(None, "dir", "elem"),
    )
    return jax.shard_map(
        on_device,
        mesh=mesh,
        in_specs=placed,
        out_specs=(P("elem"), P(None, "dir", "elem")),
        check_vma=False,
    )
```

```python
import math

import jax
import jax.numpy as jnp
from jax import lax
from jax.experimental import pallas as pl
from jax.experimental.pallas import tpu as pltpu
from jax.sharding import PartitionSpec as P

PANELS = 16384
RBANK = 4096

WAVENUM = 32.0
SOFTEN = 0.0025
TURNS = WAVENUM / (2.0 * math.pi)
MAGIC = 12582912.0

COS = (0.99999921, -19.73898036, 64.92865742, -85.27162153, 58.79049212, -21.07110563)
SIN = (6.28316113, -41.33683183, 81.44770647, -74.9094197, 33.54835515)

f32 = jnp.float32
bf16 = jnp.bfloat16


def positions(angles):
    phi = angles[0]
    psi = angles[1]
    return jnp.stack(
        [4.0 * jnp.cos(psi), jnp.sin(psi) * jnp.cos(phi), 0.6 * jnp.sin(psi) * jnp.sin(phi)]
    )


def weights(counts):
    return counts.astype(f32) * (0.5 / (4.0 * math.sqrt(PANELS)))


def lattice(index, count):
    where = index.astype(f32)
    height = 1.0 - (2.0 * where + 1.0) / count
    radius = jnp.sqrt(1.0 - height * height)
    turn = where * (math.pi * (3.0 - math.sqrt(5.0)))
    return jnp.stack([radius * jnp.cos(turn), radius * jnp.sin(turn), height])


def plane(dvec, pos):
    phase = WAVENUM * jnp.sum(dvec[:, :, None] * pos[:, None, :], axis=0)
    return jnp.stack([jnp.cos(phase), jnp.sin(phase)])


def pieces(x):
    hi = lax.reduce_precision(x, 8, 7)
    mid = lax.reduce_precision(x - hi, 8, 7)
    return hi, mid, (x - hi) - mid


def product_rows(a, b):
    ah, am, al = pieces(a)
    bh, bm, bl = pieces(b)
    left = jnp.concatenate([ah, ah, am, am, ah, al], axis=0)
    right = jnp.concatenate([bh, bm, bh, bm, bl, bh], axis=0)
    return left, right


def pad_rows(x):
    return jnp.pad(x, ((0, 32 - x.shape[0]), (0, 0))).astype(bf16)


def distance_rows(src, tgt):
    left, right = product_rows(-2.0 * src, tgt)
    ones_s = jnp.ones((3, src.shape[1]), f32)
    ones_t = jnp.ones((3, tgt.shape[1]), f32)
    sq_s = jnp.stack(pieces(jnp.sum(src * src, axis=0)))
    sq_t = jnp.stack(pieces(jnp.sum(tgt * tgt, axis=0) + SOFTEN * TURNS * TURNS))
    left = jnp.concatenate([left, sq_s, ones_s], axis=0)
    right = jnp.concatenate([right, ones_t, sq_t], axis=0)
    return pad_rows(left), pad_rows(right)


def horner(coefs, z, scale):
    total = coefs[-1] * scale
    for c in coefs[-2::-1]:
        total = total * z + c * scale
    return total


def green(d2):
    inv = lax.rsqrt(d2)
    t = d2 * inv
    r = t - ((t + MAGIC) - MAGIC)
    z = r * r
    cos_k = horner(COS, z, TURNS) * inv
    sin_k = horner(SIN, z, TURNS) * (r * inv)
    return cos_k.astype(bf16), sin_k.astype(bf16)


def mm(a, b):
    return lax.dot_general(a, b, (((1,), (0,)), ((), ())), preferred_element_type=f32)


def mt(a, b):
    return lax.dot_general(a, b, (((1,), (1,)), ((), ())), preferred_element_type=f32)


def chunk_of(total, most):
    size = min(total, most)
    while total % size:
        size //= 2
    return size


def peers_of(name):
    me = lax.axis_index(name)
    size = lax.axis_size(name)
    return [lax.rem(me + step, size) for step in range(1, size)]


def meet(*names):
    barrier = pltpu.get_barrier_semaphore()
    total = 0
    for name in names:
        for peer in peers_of(name):
            pl.semaphore_signal(
                barrier, inc=1, device_id={name: peer}, device_id_type=pl.DeviceIdType.MESH
            )
            total += 1
    pl.semaphore_wait(barrier, total)


def push(src, dst, send, recv, name, peer):
    return pltpu.make_async_remote_copy(
        src_ref=src,
        dst_ref=dst,
        send_sem=send,
        recv_sem=recv,
        device_id={name: peer},
        device_id_type=pl.DeviceIdType.MESH,
    )


def params(collective_id):
    return pltpu.CompilerParams(
        collective_id=collective_id, has_side_effects=True, vmem_limit_bytes=56 * 2**20
    )


VM = pl.BlockSpec(memory_space=pltpu.VMEM)
HBM = pl.BlockSpec(memory_space=pl.ANY)
DMA = pltpu.SemaphoreType.DMA


def gather_body(name, x_ref, o_ref, send, recv):
    me = lax.axis_index(name)
    o_ref[me] = x_ref[...]
    meet(name)
    for peer in peers_of(name):
        push(x_ref, o_ref.at[me], send.at[peer], recv.at[me], name, peer).start()
    for peer in peers_of(name):
        done = push(x_ref, o_ref.at[peer], send.at[peer], recv.at[peer], name, peer)
        done.wait_send()
        done.wait_recv()


def gather(x, name, size, collective_id):
    return pl.pallas_call(
        lambda *refs: gather_body(name, *refs),
        in_specs=[VM],
        out_specs=VM,
        out_shape=jax.ShapeDtypeStruct((size, *x.shape), x.dtype),
        scratch_shapes=[DMA((size,)), DMA((size,))],
        compiler_params=params(collective_id),
        name="gather_" + name,
    )(x)


def forward_body(
    a_ref, b_ref, v_ref,
    c_out, s_out, vg_ref, image_ref,
    c_ref, s_ref, part_ref, vb_ref, u_ref, ur_ref,
    send_a, recv_a, send_b, recv_b, send_u, recv_u, sem_c, sem_s,
):
    blocks, sub = a_ref.shape[:2]
    nb, _, tb = b_ref.shape
    groups, pair = v_ref.shape[:2]
    half = pair // 2
    lanes = groups * pair
    lag = nb // 2
    me = lax.axis_index("dir")
    spot = lax.axis_index("elem")

    def make(j, e):
        cos_k, sin_k = green(mm(a_ref[e], b_ref[j]))
        c_ref[j, e] = cos_k
        s_ref[j, e] = sin_k

    def use(j, e):
        va = vg_ref[e].reshape(lanes, sub)
        vb = vb_ref[e].reshape(lanes, sub)
        u_ref[j] += (mm(va, c_ref[j, e]) + mm(vb, s_ref[j, e])).reshape(groups, pair, tb)

    def start_out(j):
        pltpu.make_async_copy(c_ref.at[j], c_out.at[j], sem_c.at[j]).start()
        pltpu.make_async_copy(s_ref.at[j], s_out.at[j], sem_s.at[j]).start()

    def send_block(j):
        for peer in peers_of("dir"):
            push(
                u_ref.at[j, peer], ur_ref.at[me, j],
                send_u.at[peer, j], recv_u.at[me, j], "dir", peer,
            ).start()

    def make_only(j, carry):
        lax.fori_loop(0, blocks, lambda e, c: (make(j, e), c)[1], 0)
        start_out(j)
        return carry

    def both(j, carry):
        def inner(e, c):
            use(j - lag, e)
            make(j, e)
            return c

        lax.fori_loop(0, blocks, inner, 0)
        start_out(j)
        send_block(j - lag)
        return carry

    def use_only(j, carry):
        lax.fori_loop(0, blocks, lambda e, c: (use(j, e), c)[1], 0)
        send_block(j)
        return carry

    part_ref[me] = v_ref[me]
    meet("dir", "elem")
    for peer in peers_of("dir"):
        push(
            v_ref.at[peer], part_ref.at[me], send_a.at[peer], recv_a.at[me], "dir", peer
        ).start()
    u_ref[...] = jnp.zeros_like(u_ref)
    make_only(0, 0)
    for peer in peers_of("dir"):
        done = push(
            v_ref.at[peer], part_ref.at[peer], send_a.at[peer], recv_a.at[peer], "dir", peer
        )
        done.wait_send()
        done.wait_recv()
    vg_ref[spot] = part_ref[...]
    for peer in peers_of("elem"):
        push(
            part_ref, vg_ref.at[spot], send_b.at[peer], recv_b.at[spot], "elem", peer
        ).start()
    lax.fori_loop(1, lag, make_only, 0)
    for peer in peers_of("elem"):
        done = push(
            part_ref, vg_ref.at[peer], send_b.at[peer], recv_b.at[peer], "elem", peer
        )
        done.wait_send()
        done.wait_recv()
    vb_ref[:, :, :half] = -vg_ref[:, :, half:]
    vb_ref[:, :, half:] = vg_ref[:, :, :half]

    lax.fori_loop(lag, nb, both, 0)
    lax.fori_loop(nb - lag, nb, use_only, 0)

    for j in range(nb):
        total = u_ref[j, me]
        for peer in peers_of("dir"):
            done = push(
                u_ref.at[j, peer], ur_ref.at[peer, j],
                send_u.at[peer, j], recv_u.at[peer, j], "dir", peer,
            )
            done.wait_send()
            done.wait_recv()
            total += ur_ref[peer, j]
        image_ref[:, j * tb : (j + 1) * tb] = total
    for j in range(nb):
        pltpu.make_async_copy(c_ref.at[j], c_out.at[j], sem_c.at[j]).wait()
        pltpu.make_async_copy(s_ref.at[j], s_out.at[j], sem_s.at[j]).wait()


def forward(a, b, v):
    blocks, sub = a.shape[:2]
    nb, _, tb = b.shape
    groups, pair = v.shape[:2]
    table = (nb, blocks, sub, tb)
    cells = nb * blocks * sub * tb
    return pl.pallas_call(
        forward_body,
        in_specs=[VM, VM, VM],
        out_specs=[HBM, HBM, VM, VM],
        out_shape=[
            jax.ShapeDtypeStruct(table, bf16),
            jax.ShapeDtypeStruct(table, bf16),
            jax.ShapeDtypeStruct((blocks, groups, pair, sub), bf16),
            jax.ShapeDtypeStruct((pair, nb * tb), f32),
        ],
        scratch_shapes=[
            pltpu.VMEM(table, bf16),
            pltpu.VMEM(table, bf16),
            pltpu.VMEM((groups, pair, sub), bf16),
            pltpu.VMEM((blocks, groups, pair, sub), bf16),
            pltpu.VMEM((nb, groups, pair, tb), f32),
            pltpu.VMEM((groups, nb, pair, tb), f32),
            DMA((groups,)),
            DMA((groups,)),
            DMA((blocks,)),
            DMA((blocks,)),
            DMA((groups, nb)),
            DMA((groups, nb)),
            DMA((nb,)),
            DMA((nb,)),
        ],
        compiler_params=params(1),
        cost_estimate=pl.CostEstimate(
            flops=cells * 4 * groups * pair, bytes_accessed=4 * cells, transcendentals=cells
        ),
        name="forward",
    )(a, b, v)


def backward_body(
    mu_ref, c_ref, s_ref, v_ref,
    o_ref,
    ma_ref, mb_ref, g_ref, gr_ref, all_ref,
    send_m, recv_m, send_g, recv_g, send_o, recv_o,
):
    e = pl.program_id(0)
    blocks = pl.num_programs(0)
    groups, pair = ma_ref.shape[:2]
    half = pair // 2
    lanes = groups * pair
    nb, _, sub, tb = c_ref.shape
    me = lax.axis_index("dir")
    spot = lax.axis_index("elem")

    @pl.when(e == 0)
    def _():
        ma_ref[me] = mu_ref[...]
        meet("dir", "elem")
        for peer in peers_of("dir"):
            push(mu_ref, ma_ref.at[me], send_m.at[peer], recv_m.at[me], "dir", peer).start()
        for peer in peers_of("dir"):
            done = push(
                mu_ref, ma_ref.at[peer], send_m.at[peer], recv_m.at[peer], "dir", peer
            )
            done.wait_send()
            done.wait_recv()
        mb_ref[:, :half] = ma_ref[:, half:]
        mb_ref[:, half:] = -ma_ref[:, :half]

    nu = jnp.zeros((lanes, sub), f32)
    for j in range(nb):
        cols = slice(j * tb, (j + 1) * tb)
        nu += mt(ma_ref[:, :, cols].reshape(lanes, tb), c_ref[j, 0])
        nu += mt(mb_ref[:, :, cols].reshape(lanes, tb), s_ref[j, 0])
    v = v_ref[0].reshape(lanes, sub).astype(f32)
    g_ref[e] = jnp.broadcast_to(jnp.sum(nu * v, axis=0, keepdims=True), (8, sub))

    @pl.when(e == blocks - 1)
    def _():
        gr_ref[spot] = g_ref[spot]
        for peer in peers_of("elem"):
            push(
                g_ref.at[peer], gr_ref.at[spot], send_g.at[peer], recv_g.at[spot], "elem", peer
            ).start()
        for peer in peers_of("elem"):
            done = push(
                g_ref.at[peer], gr_ref.at[peer], send_g.at[peer], recv_g.at[peer], "elem", peer
            )
            done.wait_send()
            done.wait_recv()
        all_ref[me] = jnp.sum(gr_ref[...], axis=0)
        for peer in peers_of("dir"):
            push(
                all_ref.at[me], all_ref.at[me], send_o.at[peer], recv_o.at[me], "dir", peer
            ).start()
        for peer in peers_of("dir"):
            done = push(
                all_ref.at[me], all_ref.at[peer], send_o.at[peer], recv_o.at[peer], "dir", peer
            )
            done.wait_send()
            done.wait_recv()
        o_ref[...] = all_ref[...]


def backward(mu, cos_k, sin_k, v):
    nb, blocks, sub, tb = cos_k.shape
    groups, pair = v.shape[1:3]
    table = pl.BlockSpec((nb, 1, sub, tb), lambda e: (0, e, 0, 0))
    cells = cos_k.size
    return pl.pallas_call(
        backward_body,
        grid=(blocks,),
        in_specs=[VM, table, table, pl.BlockSpec((1, *v.shape[1:]), lambda e: (e, 0, 0, 0))],
        out_specs=VM,
        out_shape=jax.ShapeDtypeStruct((groups, 8, sub), f32),
        scratch_shapes=[
            pltpu.VMEM((groups, *mu.shape), bf16),
            pltpu.VMEM((groups, *mu.shape), bf16),
            pltpu.VMEM((blocks, 8, sub), f32),
            pltpu.VMEM((blocks, 8, sub), f32),
            pltpu.VMEM((groups, 8, sub), f32),
            DMA((groups,)),
            DMA((groups,)),
            DMA((blocks,)),
            DMA((blocks,)),
            DMA((groups,)),
            DMA((groups,)),
        ],
        compiler_params=params(2),
        cost_estimate=pl.CostEstimate(
            flops=cells * 4 * groups * pair, bytes_accessed=4 * cells, transcendentals=0
        ),
        name="backward",
    )(mu, cos_k, sin_k, v)


def misfit_body(x_ref, data_ref, o_ref, got_ref, send_x, recv_x, send_o, recv_o):
    me = lax.axis_index("elem")
    got_ref[me] = x_ref[me]
    meet("elem")
    for peer in peers_of("elem"):
        push(
            x_ref.at[peer], got_ref.at[me], send_x.at[peer], recv_x.at[me], "elem", peer
        ).start()
    for peer in peers_of("elem"):
        done = push(
            x_ref.at[peer], got_ref.at[peer], send_x.at[peer], recv_x.at[peer], "elem", peer
        )
        done.wait_send()
        done.wait_recv()
    o_ref[me] = (jnp.sum(got_ref[...], axis=0) - data_ref[me]).astype(bf16)
    for peer in peers_of("elem"):
        push(
            o_ref.at[me], o_ref.at[me], send_o.at[peer], recv_o.at[me], "elem", peer
        ).start()
    for peer in peers_of("elem"):
        done = push(
            o_ref.at[me], o_ref.at[peer], send_o.at[peer], recv_o.at[peer], "elem", peer
        )
        done.wait_send()
        done.wait_recv()


def far_misfit(x, data):
    blocks = x.shape[0]
    return pl.pallas_call(
        misfit_body,
        in_specs=[VM, VM],
        out_specs=VM,
        out_shape=jax.ShapeDtypeStruct(x.shape, bf16),
        scratch_shapes=[pltpu.VMEM(x.shape, f32)] + [DMA((blocks,))] * 4,
        compiler_params=params(3),
        name="far_misfit",
    )(x, data)


def table_body(rb, a_ref, b_ref, c_ref, s_ref):
    def body(k, carry):
        rows = pl.ds(pl.multiple_of(k * rb, rb), rb)
        t = mm(a_ref[rows, :], b_ref[...])
        r = t - ((t + MAGIC) - MAGIC)
        z = r * r
        c_ref[rows, :] = horner(COS, z, 1.0).astype(bf16)
        s_ref[rows, :] = (horner(SIN, z, 1.0) * r).astype(bf16)
        return carry

    lax.fori_loop(0, a_ref.shape[0] // rb, body, 0)


def far_table(a, b):
    rows = a.shape[0]
    recv = b.shape[1]
    tb = chunk_of(recv, 256)
    rb = chunk_of(rows, 256)
    col = lambda n: pl.BlockSpec((n, tb), lambda i: (0, i))
    out = jax.ShapeDtypeStruct((rows, recv), bf16)
    cells = rows * recv
    return pl.pallas_call(
        lambda *refs: table_body(rb, *refs),
        grid=(recv // tb,),
        in_specs=[pl.BlockSpec(a.shape, lambda i: (0, 0)), col(32)],
        out_specs=[col(rows), col(rows)],
        out_shape=[out, out],
        compiler_params=pltpu.CompilerParams(vmem_limit_bytes=48 * 2**20),
        cost_estimate=pl.CostEstimate(flops=cells * 30, bytes_accessed=4 * cells, transcendentals=0),
        name="far_table",
    )(a, b)


def apply(vec, cos_t, sin_t, sign, axis):
    half = vec.shape[1]
    stacked = vec.reshape(2 * half, vec.shape[2])
    dims = (((1,), (axis,)), ((), ()))
    first = lax.dot_general(stacked, cos_t, dims, preferred_element_type=f32)
    second = lax.dot_general(stacked, sin_t, dims, preferred_element_type=f32)
    real = first[:half] - sign * second[half:]
    imag = first[half:] + sign * second[:half]
    return jnp.stack([real, imag])


def on_device(panel_angles, impedance, quad_count, receivers, farfield_data, warm_density):
    rows = impedance.shape[0]
    count_dir = farfield_data.shape[1]
    groups = lax.axis_size("dir")
    blocks = lax.axis_size("elem")
    ndir = count_dir * groups
    sub = rows // groups
    me = lax.axis_index("dir")

    w_loc = weights(quad_count)
    wz_loc = w_loc * impedance
    pos_loc = positions(panel_angles)
    turn_loc = pos_loc * TURNS

    src = lax.dynamic_slice_in_dim(turn_loc, me * sub, sub, 1)
    src = gather(jnp.pad(src, ((0, 5), (0, 0))), "elem", blocks, 0)
    src = jnp.transpose(src[:, :3], (1, 0, 2)).reshape(3, blocks * sub)
    v = (wz_loc * warm_density).astype(bf16)
    v = jnp.transpose(v.reshape(2 * count_dir, groups, sub), (1, 0, 2))

    left, right = distance_rows(src, turn_loc)
    tb = chunk_of(rows, 256)
    left = left.T.reshape(blocks, sub, left.shape[0])
    right = jnp.transpose(right.reshape(right.shape[0], rows // tb, tb), (1, 0, 2))
    cos_k, sin_k, v_all, image = forward(left, right, v)
    image = image.reshape(2, count_dir, rows)

    dvec = lattice(me * count_dir + jnp.arange(count_dir, dtype=jnp.int32), ndir)
    state = plane(dvec, pos_loc) - image

    left, right = product_rows(turn_loc, lattice(receivers, RBANK))
    cos_t, sin_t = far_table(pad_rows(left).T, pad_rows(right))
    partial_far = apply((w_loc * state).astype(bf16), cos_t, sin_t, -1.0, 0)
    pair = 2 * count_dir
    recv = farfield_data.shape[2]

    def split(x):
        return jnp.transpose(x.reshape(pair, blocks, recv // blocks), (1, 0, 2))

    misfit = far_misfit(split(partial_far), split(farfield_data))
    misfit = jnp.transpose(misfit, (1, 0, 2)).reshape(2, count_dir, recv)
    adjoint = (w_loc * apply(misfit, cos_t, sin_t, 1.0, 1)).astype(bf16)

    grad = backward(adjoint.reshape(pair, rows), cos_k, sin_k, v_all)
    return (grad[:, 0].reshape(rows) / (-ndir * wz_loc), state)


def solution(mesh):
    placed = (
        P(None, "elem"),
        P("elem"),
        P("elem"),
        P(),
        P(None, "dir", None),
        P(None, "dir", "elem"),
    )
    return jax.shard_map(
        on_device,
        mesh=mesh,
        in_specs=placed,
        out_specs=(P("elem"), P(None, "dir", "elem")),
        check_vma=False,
    )
```

```python
import math

import jax
import jax.numpy as jnp
from jax import lax
from jax.experimental import pallas as pl
from jax.experimental.pallas import tpu as pltpu
from jax.sharding import PartitionSpec as P

PANELS = 16384
RBANK = 4096

WAVENUM = 32.0
SOFTEN = 0.0025
TURNS = WAVENUM / (2.0 * math.pi)
MAGIC = 12582912.0

COS = (0.99999921, -19.73898036, 64.92865742, -85.27162153, 58.79049212, -21.07110563)
SIN = (6.28316113, -41.33683183, 81.44770647, -74.9094197, 33.54835515)

f32 = jnp.float32
bf16 = jnp.bfloat16


def positions(angles):
    phi = angles[0]
    psi = angles[1]
    return jnp.stack(
        [4.0 * jnp.cos(psi), jnp.sin(psi) * jnp.cos(phi), 0.6 * jnp.sin(psi) * jnp.sin(phi)]
    )


def weights(counts):
    return counts.astype(f32) * (0.5 / (4.0 * math.sqrt(PANELS)))


def lattice(index, count):
    where = index.astype(f32)
    height = 1.0 - (2.0 * where + 1.0) / count
    radius = jnp.sqrt(1.0 - height * height)
    turn = where * (math.pi * (3.0 - math.sqrt(5.0)))
    return jnp.stack([radius * jnp.cos(turn), radius * jnp.sin(turn), height])


def plane(dvec, pos):
    phase = WAVENUM * jnp.sum(dvec[:, :, None] * pos[:, None, :], axis=0)
    return jnp.stack([jnp.cos(phase), jnp.sin(phase)])


def pieces(x):
    hi = lax.reduce_precision(x, 8, 7)
    mid = lax.reduce_precision(x - hi, 8, 7)
    return hi, mid, (x - hi) - mid


def product_rows(a, b):
    ah, am, al = pieces(a)
    bh, bm, bl = pieces(b)
    left = jnp.concatenate([ah, ah, am, am, ah, al], axis=0)
    right = jnp.concatenate([bh, bm, bh, bm, bl, bh], axis=0)
    return left, right


def pad_rows(x):
    return jnp.pad(x, ((0, 32 - x.shape[0]), (0, 0))).astype(bf16)


def distance_rows(src, tgt):
    left, right = product_rows(-2.0 * src, tgt)
    ones_s = jnp.ones((3, src.shape[1]), f32)
    ones_t = jnp.ones((3, tgt.shape[1]), f32)
    sq_s = jnp.stack(pieces(jnp.sum(src * src, axis=0)))
    sq_t = jnp.stack(pieces(jnp.sum(tgt * tgt, axis=0) + SOFTEN * TURNS * TURNS))
    left = jnp.concatenate([left, sq_s, ones_s], axis=0)
    right = jnp.concatenate([right, ones_t, sq_t], axis=0)
    return pad_rows(left), pad_rows(right)


def monic(coefs, z):
    total = z + coefs[-2] / coefs[-1]
    for c in coefs[-3::-1]:
        total = total * z + c / coefs[-1]
    return total


def fraction(t):
    return t - ((t + MAGIC) - MAGIC)


def green(d2):
    inv = lax.rsqrt(d2)
    r = fraction(d2 * inv)
    z = r * r
    cos_k = monic(COS, z) * inv
    sin_k = monic(SIN, z) * (r * inv)
    return cos_k.astype(bf16), sin_k.astype(bf16)


def strips(rows):
    step = min(rows, 32)
    return [slice(i, i + step) for i in range(0, rows, step)]


def mm(a, b):
    return lax.dot_general(a, b, (((1,), (0,)), ((), ())), preferred_element_type=f32)


def chunk_of(total, most):
    size = min(total, most)
    while total % size:
        size //= 2
    return size


def peers_of(name):
    me = lax.axis_index(name)
    size = lax.axis_size(name)
    return [lax.rem(me + step, size) for step in range(1, size)]


def meet(*names):
    barrier = pltpu.get_barrier_semaphore()
    total = 0
    for name in names:
        for peer in peers_of(name):
            pl.semaphore_signal(
                barrier, inc=1, device_id={name: peer}, device_id_type=pl.DeviceIdType.MESH
            )
            total += 1
    pl.semaphore_wait(barrier, total)


def push(src, dst, send, recv, name, peer):
    return pltpu.make_async_remote_copy(
        src_ref=src,
        dst_ref=dst,
        send_sem=send,
        recv_sem=recv,
        device_id={name: peer},
        device_id_type=pl.DeviceIdType.MESH,
    )


def params(collective_id):
    return pltpu.CompilerParams(
        collective_id=collective_id, has_side_effects=True, vmem_limit_bytes=56 * 2**20
    )


VM = pl.BlockSpec(memory_space=pltpu.VMEM)
HBM = pl.BlockSpec(memory_space=pl.ANY)
DMA = pltpu.SemaphoreType.DMA


def forward_body(
    a_ref, b_ref, v_ref,
    c_out, s_out, vg_ref, image_ref,
    c_ref, s_ref, geo_ref, at_ref, part_ref, vb_ref, u_ref, ur_ref,
    send_x, recv_x, send_a, recv_a, send_b, recv_b, send_u, recv_u, sem_c, sem_s,
):
    blocks, sub = at_ref.shape[:2]
    nb, _, tb = b_ref.shape
    groups, pair = v_ref.shape[:2]
    half = pair // 2
    lanes = groups * pair
    lag = nb // 2
    me = lax.axis_index("dir")
    spot = lax.axis_index("elem")

    def make(j, e):
        d2 = mm(at_ref[e], b_ref[j])
        for strip in strips(sub):
            cos_k, sin_k = green(d2[strip])
            c_ref[j, e, strip, :] = cos_k
            s_ref[j, e, strip, :] = sin_k

    def use(j, e):
        va = vg_ref[e].reshape(lanes, sub)
        vb = vb_ref[e].reshape(lanes, sub)
        total = (TURNS * COS[-1]) * mm(va, c_ref[j, e]) + (TURNS * SIN[-1]) * mm(vb, s_ref[j, e])
        u_ref[j] += total.reshape(groups, pair, tb)

    def start_out(j):
        pltpu.make_async_copy(c_ref.at[j], c_out.at[j], sem_c.at[j]).start()
        pltpu.make_async_copy(s_ref.at[j], s_out.at[j], sem_s.at[j]).start()

    def send_block(j):
        for peer in peers_of("dir"):
            push(
                u_ref.at[j, peer], ur_ref.at[me, j],
                send_u.at[peer, j], recv_u.at[me, j], "dir", peer,
            ).start()

    def make_only(j, carry):
        lax.fori_loop(0, blocks, lambda e, c: (make(j, e), c)[1], 0)
        start_out(j)
        return carry

    def both(j, carry):
        def inner(e, c):
            use(j - lag, e)
            make(j, e)
            return c

        lax.fori_loop(0, blocks, inner, 0)
        start_out(j)
        send_block(j - lag)
        return carry

    def use_only(j, carry):
        lax.fori_loop(0, blocks, lambda e, c: (use(j, e), c)[1], 0)
        send_block(j)
        return carry

    part_ref[me] = v_ref[me]
    geo_ref[spot] = a_ref[...]
    meet("dir", "elem")
    for peer in peers_of("elem"):
        push(
            a_ref, geo_ref.at[spot], send_x.at[peer], recv_x.at[spot], "elem", peer
        ).start()
    for peer in peers_of("dir"):
        push(
            v_ref.at[peer], part_ref.at[me], send_a.at[peer], recv_a.at[me], "dir", peer
        ).start()
    u_ref[...] = jnp.zeros_like(u_ref)
    for peer in peers_of("elem"):
        done = push(a_ref, geo_ref.at[peer], send_x.at[peer], recv_x.at[peer], "elem", peer)
        done.wait_send()
        done.wait_recv()
    for e in range(blocks):
        at_ref[e] = geo_ref[e].astype(f32).T.astype(bf16)
    make_only(0, 0)
    for peer in peers_of("dir"):
        done = push(
            v_ref.at[peer], part_ref.at[peer], send_a.at[peer], recv_a.at[peer], "dir", peer
        )
        done.wait_send()
        done.wait_recv()
    vg_ref[spot] = part_ref[...]
    for peer in peers_of("elem"):
        push(
            part_ref, vg_ref.at[spot], send_b.at[peer], recv_b.at[spot], "elem", peer
        ).start()
    lax.fori_loop(1, lag, make_only, 0)
    for peer in peers_of("elem"):
        done = push(
            part_ref, vg_ref.at[peer], send_b.at[peer], recv_b.at[peer], "elem", peer
        )
        done.wait_send()
        done.wait_recv()
    vb_ref[:, :, :half] = -vg_ref[:, :, half:]
    vb_ref[:, :, half:] = vg_ref[:, :, :half]

    lax.fori_loop(lag, nb, both, 0)
    lax.fori_loop(nb - lag, nb, use_only, 0)

    for j in range(nb):
        total = u_ref[j, me]
        for peer in peers_of("dir"):
            done = push(
                u_ref.at[j, peer], ur_ref.at[peer, j],
                send_u.at[peer, j], recv_u.at[peer, j], "dir", peer,
            )
            done.wait_send()
            done.wait_recv()
            total += ur_ref[peer, j]
        image_ref[:, j * tb : (j + 1) * tb] = total
    for j in range(nb):
        pltpu.make_async_copy(c_ref.at[j], c_out.at[j], sem_c.at[j]).wait()
        pltpu.make_async_copy(s_ref.at[j], s_out.at[j], sem_s.at[j]).wait()


def forward(a, b, v, blocks):
    sub = a.shape[1]
    nb, _, tb = b.shape
    groups, pair = v.shape[:2]
    table = (nb, blocks, sub, tb)
    cells = nb * blocks * sub * tb
    return pl.pallas_call(
        forward_body,
        in_specs=[VM, VM, VM],
        out_specs=[HBM, HBM, VM, VM],
        out_shape=[
            jax.ShapeDtypeStruct(table, bf16),
            jax.ShapeDtypeStruct(table, bf16),
            jax.ShapeDtypeStruct((blocks, groups, pair, sub), bf16),
            jax.ShapeDtypeStruct((pair, nb * tb), f32),
        ],
        scratch_shapes=[
            pltpu.VMEM(table, bf16),
            pltpu.VMEM(table, bf16),
            pltpu.VMEM((blocks, *a.shape), bf16),
            pltpu.VMEM((blocks, sub, a.shape[0]), bf16),
            pltpu.VMEM((groups, pair, sub), bf16),
            pltpu.VMEM((blocks, groups, pair, sub), bf16),
            pltpu.VMEM((nb, groups, pair, tb), f32),
            pltpu.VMEM((groups, nb, pair, tb), f32),
            DMA((blocks,)),
            DMA((blocks,)),
            DMA((groups,)),
            DMA((groups,)),
            DMA((blocks,)),
            DMA((blocks,)),
            DMA((groups, nb)),
            DMA((groups, nb)),
            DMA((nb,)),
            DMA((nb,)),
        ],
        compiler_params=params(1),
        cost_estimate=pl.CostEstimate(
            flops=cells * 4 * groups * pair, bytes_accessed=4 * cells, transcendentals=cells
        ),
        name="forward",
    )(a, b, v)


def backward_body(
    mu_ref, c_ref, s_ref, v_ref,
    o_ref,
    ma_ref, mat_ref, mbt_ref, g_ref, gr_ref, all_ref,
    send_m, recv_m, send_g, recv_g, send_o, recv_o,
):
    e = pl.program_id(0)
    blocks = pl.num_programs(0)
    groups, pair = ma_ref.shape[:2]
    half = pair // 2
    lanes = groups * pair
    nb, _, sub, tb = c_ref.shape
    me = lax.axis_index("dir")
    spot = lax.axis_index("elem")

    @pl.when(e == 0)
    def _():
        ma_ref[me] = mu_ref[...]
        meet("dir", "elem")
        for peer in peers_of("dir"):
            push(mu_ref, ma_ref.at[me], send_m.at[peer], recv_m.at[me], "dir", peer).start()
        for peer in peers_of("dir"):
            done = push(
                mu_ref, ma_ref.at[peer], send_m.at[peer], recv_m.at[peer], "dir", peer
            )
            done.wait_send()
            done.wait_recv()
        for j in range(nb):
            cols = slice(j * tb, (j + 1) * tb)
            ma = ma_ref[:, :, cols].astype(f32)
            mb = jnp.concatenate([ma[:, half:], -ma[:, :half]], axis=1)
            mat_ref[j] = ma.reshape(lanes, tb).T.astype(bf16)
            mbt_ref[j] = mb.reshape(lanes, tb).T.astype(bf16)

    first = mm(c_ref[0, 0], mat_ref[0])
    second = mm(s_ref[0, 0], mbt_ref[0])
    for j in range(1, nb):
        first += mm(c_ref[j, 0], mat_ref[j])
        second += mm(s_ref[j, 0], mbt_ref[j])
    nu = ((TURNS * COS[-1]) * first + (TURNS * SIN[-1]) * second).T
    v = v_ref[0].reshape(lanes, sub).astype(f32)
    g_ref[e] = jnp.broadcast_to(jnp.sum(nu * v, axis=0, keepdims=True), (8, sub))

    @pl.when(e == blocks - 1)
    def _():
        gr_ref[spot] = g_ref[spot]
        for peer in peers_of("elem"):
            push(
                g_ref.at[peer], gr_ref.at[spot], send_g.at[peer], recv_g.at[spot], "elem", peer
            ).start()
        for peer in peers_of("elem"):
            done = push(
                g_ref.at[peer], gr_ref.at[peer], send_g.at[peer], recv_g.at[peer], "elem", peer
            )
            done.wait_send()
            done.wait_recv()
        all_ref[me] = jnp.sum(gr_ref[...], axis=0)
        for peer in peers_of("dir"):
            push(
                all_ref.at[me], all_ref.at[me], send_o.at[peer], recv_o.at[me], "dir", peer
            ).start()
        for peer in peers_of("dir"):
            done = push(
                all_ref.at[me], all_ref.at[peer], send_o.at[peer], recv_o.at[peer], "dir", peer
            )
            done.wait_send()
            done.wait_recv()
        o_ref[...] = all_ref[...]


def backward(mu, cos_k, sin_k, v):
    nb, blocks, sub, tb = cos_k.shape
    groups, pair = v.shape[1:3]
    table = pl.BlockSpec((nb, 1, sub, tb), lambda e: (0, e, 0, 0))
    cells = cos_k.size
    return pl.pallas_call(
        backward_body,
        grid=(blocks,),
        in_specs=[VM, table, table, pl.BlockSpec((1, *v.shape[1:]), lambda e: (e, 0, 0, 0))],
        out_specs=VM,
        out_shape=jax.ShapeDtypeStruct((groups, 8, sub), f32),
        scratch_shapes=[
            pltpu.VMEM((groups, *mu.shape), bf16),
            pltpu.VMEM((nb, tb, groups * pair), bf16),
            pltpu.VMEM((nb, tb, groups * pair), bf16),
            pltpu.VMEM((blocks, 8, sub), f32),
            pltpu.VMEM((blocks, 8, sub), f32),
            pltpu.VMEM((groups, 8, sub), f32),
            DMA((groups,)),
            DMA((groups,)),
            DMA((blocks,)),
            DMA((blocks,)),
            DMA((groups,)),
            DMA((groups,)),
        ],
        compiler_params=params(2),
        cost_estimate=pl.CostEstimate(
            flops=cells * 4 * groups * pair, bytes_accessed=4 * cells, transcendentals=0
        ),
        name="backward",
    )(mu, cos_k, sin_k, v)


def misfit_body(x_ref, data_ref, o_ref, got_ref, send_x, recv_x, send_o, recv_o):
    me = lax.axis_index("elem")
    got_ref[me] = x_ref[me]
    meet("elem")
    for peer in peers_of("elem"):
        push(
            x_ref.at[peer], got_ref.at[me], send_x.at[peer], recv_x.at[me], "elem", peer
        ).start()
    for peer in peers_of("elem"):
        done = push(
            x_ref.at[peer], got_ref.at[peer], send_x.at[peer], recv_x.at[peer], "elem", peer
        )
        done.wait_send()
        done.wait_recv()
    o_ref[me] = (jnp.sum(got_ref[...], axis=0) - data_ref[me]).astype(bf16)
    for peer in peers_of("elem"):
        push(
            o_ref.at[me], o_ref.at[me], send_o.at[peer], recv_o.at[me], "elem", peer
        ).start()
    for peer in peers_of("elem"):
        done = push(
            o_ref.at[me], o_ref.at[peer], send_o.at[peer], recv_o.at[peer], "elem", peer
        )
        done.wait_send()
        done.wait_recv()


def far_misfit(x, data):
    blocks = x.shape[0]
    return pl.pallas_call(
        misfit_body,
        in_specs=[VM, VM],
        out_specs=VM,
        out_shape=jax.ShapeDtypeStruct(x.shape, bf16),
        scratch_shapes=[pltpu.VMEM(x.shape, f32)] + [DMA((blocks,))] * 4,
        compiler_params=params(3),
        name="far_misfit",
    )(x, data)


def table_body(rb, a_ref, b_ref, c_ref, s_ref):
    def body(k, carry):
        rows = pl.ds(pl.multiple_of(k * rb, rb), rb)
        t = mm(a_ref[rows, :], b_ref[...])
        for strip in strips(rb):
            r = fraction(t[strip])
            z = r * r
            part = pl.ds(pl.multiple_of(k * rb + strip.start, strip.stop - strip.start), strip.stop - strip.start)
            c_ref[part, :] = monic(COS, z).astype(bf16)
            s_ref[part, :] = (monic(SIN, z) * r).astype(bf16)
        return carry

    lax.fori_loop(0, a_ref.shape[0] // rb, body, 0)


def far_table(a, b):
    rows = a.shape[0]
    recv = b.shape[1]
    tb = chunk_of(recv, 256)
    rb = chunk_of(rows, 256)
    col = lambda n: pl.BlockSpec((n, tb), lambda i: (0, i))
    out = jax.ShapeDtypeStruct((rows, recv), bf16)
    cells = rows * recv
    return pl.pallas_call(
        lambda *refs: table_body(rb, *refs),
        grid=(recv // tb,),
        in_specs=[pl.BlockSpec(a.shape, lambda i: (0, 0)), col(32)],
        out_specs=[col(rows), col(rows)],
        out_shape=[out, out],
        compiler_params=pltpu.CompilerParams(vmem_limit_bytes=48 * 2**20),
        cost_estimate=pl.CostEstimate(flops=cells * 30, bytes_accessed=4 * cells, transcendentals=0),
        name="far_table",
    )(a, b)


def apply(vec, cos_t, sin_t, sign, axis):
    half = vec.shape[1]
    stacked = vec.reshape(2 * half, vec.shape[2])
    dims = (((1,), (axis,)), ((), ()))
    first = COS[-1] * lax.dot_general(stacked, cos_t, dims, preferred_element_type=f32)
    second = SIN[-1] * lax.dot_general(stacked, sin_t, dims, preferred_element_type=f32)
    real = first[:half] - sign * second[half:]
    imag = first[half:] + sign * second[:half]
    return jnp.stack([real, imag])


def on_device(panel_angles, impedance, quad_count, receivers, farfield_data, warm_density):
    rows = impedance.shape[0]
    count_dir = farfield_data.shape[1]
    groups = lax.axis_size("dir")
    blocks = lax.axis_size("elem")
    ndir = count_dir * groups
    sub = rows // groups
    me = lax.axis_index("dir")

    w_loc = weights(quad_count)
    wz_loc = w_loc * impedance
    pos_loc = positions(panel_angles)
    turn_loc = pos_loc * TURNS

    src = lax.dynamic_slice_in_dim(turn_loc, me * sub, sub, 1)
    v = (wz_loc * warm_density).astype(bf16)
    v = jnp.transpose(v.reshape(2 * count_dir, groups, sub), (1, 0, 2))

    left, right = distance_rows(src, turn_loc)
    tb = chunk_of(rows, 256)
    right = jnp.transpose(right.reshape(right.shape[0], rows // tb, tb), (1, 0, 2))
    cos_k, sin_k, v_all, image = forward(left, right, v, blocks)
    image = image.reshape(2, count_dir, rows)

    dvec = lattice(me * count_dir + jnp.arange(count_dir, dtype=jnp.int32), ndir)
    state = plane(dvec, pos_loc) - image

    left, right = product_rows(turn_loc, lattice(receivers, RBANK))
    cos_t, sin_t = far_table(pad_rows(left).T, pad_rows(right))
    partial_far = apply((w_loc * state).astype(bf16), cos_t, sin_t, -1.0, 0)
    pair = 2 * count_dir
    recv = farfield_data.shape[2]

    def split(x):
        return jnp.transpose(x.reshape(pair, blocks, recv // blocks), (1, 0, 2))

    misfit = far_misfit(split(partial_far), split(farfield_data))
    misfit = jnp.transpose(misfit, (1, 0, 2)).reshape(2, count_dir, recv)
    adjoint = (w_loc * apply(misfit, cos_t, sin_t, 1.0, 1)).astype(bf16)

    grad = backward(adjoint.reshape(pair, rows), cos_k, sin_k, v_all)
    return (grad[:, 0].reshape(rows) / (-ndir * wz_loc), state)


def solution(mesh):
    placed = (
        P(None, "elem"),
        P("elem"),
        P("elem"),
        P(),
        P(None, "dir", None),
        P(None, "dir", "elem"),
    )
    return jax.shard_map(
        on_device,
        mesh=mesh,
        in_specs=placed,
        out_specs=(P("elem"), P(None, "dir", "elem")),
        check_vma=False,
    )
```

```python
import math

import jax
import jax.numpy as jnp
from jax import lax
from jax.experimental import pallas as pl
from jax.experimental.pallas import tpu as pltpu
from jax.sharding import PartitionSpec as P

PANELS = 16384
RBANK = 4096

WAVENUM = 32.0
SOFTEN = 0.0025
TURNS = WAVENUM / (2.0 * math.pi)
MAGIC = 12582912.0

COS = (0.99999921, -19.73898036, 64.92865742, -85.27162153, 58.79049212, -21.07110563)
SIN = (6.28316113, -41.33683183, 81.44770647, -74.9094197, 33.54835515)

f32 = jnp.float32
bf16 = jnp.bfloat16


def positions(angles):
    phi = angles[0]
    psi = angles[1]
    return jnp.stack(
        [4.0 * jnp.cos(psi), jnp.sin(psi) * jnp.cos(phi), 0.6 * jnp.sin(psi) * jnp.sin(phi)]
    )


def weights(counts):
    return counts.astype(f32) * (0.5 / (4.0 * math.sqrt(PANELS)))


def lattice(index, count):
    where = index.astype(f32)
    height = 1.0 - (2.0 * where + 1.0) / count
    radius = jnp.sqrt(1.0 - height * height)
    turn = where * (math.pi * (3.0 - math.sqrt(5.0)))
    return jnp.stack([radius * jnp.cos(turn), radius * jnp.sin(turn), height])


def plane(dvec, pos):
    phase = WAVENUM * jnp.sum(dvec[:, :, None] * pos[:, None, :], axis=0)
    return jnp.stack([jnp.cos(phase), jnp.sin(phase)])


def pieces(x):
    hi = lax.reduce_precision(x, 8, 7)
    mid = lax.reduce_precision(x - hi, 8, 7)
    return hi, mid, (x - hi) - mid


def product_rows(a, b):
    ah, am, al = pieces(a)
    bh, bm, bl = pieces(b)
    left = jnp.concatenate([ah, ah, am, am, ah, al], axis=0)
    right = jnp.concatenate([bh, bm, bh, bm, bl, bh], axis=0)
    return left, right


def pad_rows(x):
    return jnp.pad(x, ((0, 32 - x.shape[0]), (0, 0))).astype(bf16)


def distance_rows(src, tgt):
    left, right = product_rows(-2.0 * src, tgt)
    ones_s = jnp.ones((3, src.shape[1]), f32)
    ones_t = jnp.ones((3, tgt.shape[1]), f32)
    sq_s = jnp.stack(pieces(jnp.sum(src * src, axis=0)))
    sq_t = jnp.stack(pieces(jnp.sum(tgt * tgt, axis=0) + SOFTEN * TURNS * TURNS))
    left = jnp.concatenate([left, sq_s, ones_s], axis=0)
    right = jnp.concatenate([right, ones_t, sq_t], axis=0)
    return pad_rows(left), pad_rows(right)


def monic(coefs, z):
    total = z + coefs[-2] / coefs[-1]
    for c in coefs[-3::-1]:
        total = total * z + c / coefs[-1]
    return total


def fraction(t):
    return t - ((t + MAGIC) - MAGIC)


def green(d2):
    inv = lax.rsqrt(d2)
    r = fraction(d2 * inv)
    z = r * r
    cos_k = monic(COS, z) * inv
    sin_k = monic(SIN, z) * (r * inv)
    return cos_k.astype(bf16), sin_k.astype(bf16)


def strips(rows):
    step = min(rows, 32)
    return [slice(i, i + step) for i in range(0, rows, step)]


def mm(a, b):
    return lax.dot_general(a, b, (((1,), (0,)), ((), ())), preferred_element_type=f32)


def mt(a, b):
    return lax.dot_general(a, b, (((1,), (1,)), ((), ())), preferred_element_type=f32)


def chunk_of(total, most):
    size = min(total, most)
    while total % size:
        size //= 2
    return size


def peers_of(name):
    me = lax.axis_index(name)
    size = lax.axis_size(name)
    return [lax.rem(me + step, size) for step in range(1, size)]


def meet(*names):
    barrier = pltpu.get_barrier_semaphore()
    total = 0
    for name in names:
        for peer in peers_of(name):
            pl.semaphore_signal(
                barrier, inc=1, device_id={name: peer}, device_id_type=pl.DeviceIdType.MESH
            )
            total += 1
    pl.semaphore_wait(barrier, total)


def push(src, dst, send, recv, name, peer):
    return pltpu.make_async_remote_copy(
        src_ref=src,
        dst_ref=dst,
        send_sem=send,
        recv_sem=recv,
        device_id={name: peer},
        device_id_type=pl.DeviceIdType.MESH,
    )


def params(collective_id):
    return pltpu.CompilerParams(
        collective_id=collective_id, has_side_effects=True, vmem_limit_bytes=56 * 2**20
    )


VM = pl.BlockSpec(memory_space=pltpu.VMEM)
HBM = pl.BlockSpec(memory_space=pl.ANY)
DMA = pltpu.SemaphoreType.DMA


def forward_body(
    a_ref, b_ref, v_ref,
    c_out, s_out, vg_ref, image_ref,
    c_ref, s_ref, geo_ref, at_ref, part_ref, vb_ref, u_ref, ur_ref,
    send_x, recv_x, send_a, recv_a, send_b, recv_b, send_u, recv_u, sem_c, sem_s,
):
    blocks, sub = at_ref.shape[:2]
    nb, _, tb = b_ref.shape
    groups, pair = v_ref.shape[:2]
    half = pair // 2
    lanes = groups * pair
    lag = nb // 2
    me = lax.axis_index("dir")
    spot = lax.axis_index("elem")

    def make(j, e):
        d2 = mm(at_ref[e], b_ref[j])
        for strip in strips(sub):
            cos_k, sin_k = green(d2[strip])
            c_ref[j, e, strip, :] = cos_k
            s_ref[j, e, strip, :] = sin_k

    def use(j, e):
        va = vg_ref[e].reshape(lanes, sub)
        vb = vb_ref[e].reshape(lanes, sub)
        total = (TURNS * COS[-1]) * mm(va, c_ref[j, e]) + (TURNS * SIN[-1]) * mm(vb, s_ref[j, e])
        u_ref[j] += total.reshape(groups, pair, tb)

    def start_out(j):
        pltpu.make_async_copy(c_ref.at[j], c_out.at[j], sem_c.at[j]).start()
        pltpu.make_async_copy(s_ref.at[j], s_out.at[j], sem_s.at[j]).start()

    def send_block(j):
        for peer in peers_of("dir"):
            push(
                u_ref.at[j, peer], ur_ref.at[me, j],
                send_u.at[peer, j], recv_u.at[me, j], "dir", peer,
            ).start()

    def others(act):
        at = lambda i: lax.rem(spot + i, blocks)

        def two(i, c):
            act([at(2 * i + 1), at(2 * i + 2)])
            return c

        pairs = (blocks - 1) // 2
        lax.fori_loop(0, pairs, two, 0)
        if blocks - 1 > 2 * pairs:
            act([at(blocks - 1)])

    def make_only(j, carry):
        others(lambda es: [make(j, e) for e in es])
        start_out(j)
        return carry

    def both(j, carry):
        others(lambda es: [use(j - lag, e) for e in es] + [make(j, e) for e in es])
        use(j - lag, spot)
        start_out(j)
        send_block(j - lag)
        return carry

    def use_only(j, carry):
        lax.fori_loop(0, blocks, lambda e, c: (use(j, e), c)[1], 0)
        send_block(j)
        return carry

    part_ref[me] = v_ref[me]
    geo_ref[spot] = a_ref[...]
    meet("dir", "elem")
    for peer in peers_of("elem"):
        push(
            a_ref, geo_ref.at[spot], send_x.at[peer], recv_x.at[spot], "elem", peer
        ).start()
    for peer in peers_of("dir"):
        push(
            v_ref.at[peer], part_ref.at[me], send_a.at[peer], recv_a.at[me], "dir", peer
        ).start()
    u_ref[...] = jnp.zeros_like(u_ref)
    at_ref[spot] = a_ref[...].astype(f32).T.astype(bf16)

    def make_own(j, carry):
        make(j, spot)
        return carry

    lax.fori_loop(0, nb, make_own, 0)
    for peer in peers_of("elem"):
        done = push(a_ref, geo_ref.at[peer], send_x.at[peer], recv_x.at[peer], "elem", peer)
        done.wait_send()
        done.wait_recv()
    for e in range(blocks):
        at_ref[e] = geo_ref[e].astype(f32).T.astype(bf16)
    make_only(0, 0)
    for peer in peers_of("dir"):
        done = push(
            v_ref.at[peer], part_ref.at[peer], send_a.at[peer], recv_a.at[peer], "dir", peer
        )
        done.wait_send()
        done.wait_recv()
    vg_ref[spot] = part_ref[...]
    for peer in peers_of("elem"):
        push(
            part_ref, vg_ref.at[spot], send_b.at[peer], recv_b.at[spot], "elem", peer
        ).start()
    lax.fori_loop(1, lag, make_only, 0)
    for peer in peers_of("elem"):
        done = push(
            part_ref, vg_ref.at[peer], send_b.at[peer], recv_b.at[peer], "elem", peer
        )
        done.wait_send()
        done.wait_recv()
    vb_ref[:, :, :half] = -vg_ref[:, :, half:]
    vb_ref[:, :, half:] = vg_ref[:, :, :half]

    lax.fori_loop(lag, nb, both, 0)
    lax.fori_loop(nb - lag, nb, use_only, 0)

    for j in range(nb):
        total = u_ref[j, me]
        for peer in peers_of("dir"):
            done = push(
                u_ref.at[j, peer], ur_ref.at[peer, j],
                send_u.at[peer, j], recv_u.at[peer, j], "dir", peer,
            )
            done.wait_send()
            done.wait_recv()
            total += ur_ref[peer, j]
        image_ref[:, j * tb : (j + 1) * tb] = total
    for j in range(nb):
        pltpu.make_async_copy(c_ref.at[j], c_out.at[j], sem_c.at[j]).wait()
        pltpu.make_async_copy(s_ref.at[j], s_out.at[j], sem_s.at[j]).wait()


def forward(a, b, v, blocks):
    sub = a.shape[1]
    nb, _, tb = b.shape
    groups, pair = v.shape[:2]
    table = (nb, blocks, sub, tb)
    cells = nb * blocks * sub * tb
    return pl.pallas_call(
        forward_body,
        in_specs=[VM, VM, VM],
        out_specs=[HBM, HBM, VM, VM],
        out_shape=[
            jax.ShapeDtypeStruct(table, bf16),
            jax.ShapeDtypeStruct(table, bf16),
            jax.ShapeDtypeStruct((blocks, groups, pair, sub), bf16),
            jax.ShapeDtypeStruct((pair, nb * tb), f32),
        ],
        scratch_shapes=[
            pltpu.VMEM(table, bf16),
            pltpu.VMEM(table, bf16),
            pltpu.VMEM((blocks, *a.shape), bf16),
            pltpu.VMEM((blocks, sub, a.shape[0]), bf16),
            pltpu.VMEM((groups, pair, sub), bf16),
            pltpu.VMEM((blocks, groups, pair, sub), bf16),
            pltpu.VMEM((nb, groups, pair, tb), f32),
            pltpu.VMEM((groups, nb, pair, tb), f32),
            DMA((blocks,)),
            DMA((blocks,)),
            DMA((groups,)),
            DMA((groups,)),
            DMA((blocks,)),
            DMA((blocks,)),
            DMA((groups, nb)),
            DMA((groups, nb)),
            DMA((nb,)),
            DMA((nb,)),
        ],
        compiler_params=params(1),
        cost_estimate=pl.CostEstimate(
            flops=cells * 4 * groups * pair, bytes_accessed=4 * cells, transcendentals=cells
        ),
        name="forward",
    )(a, b, v)


def backward_body(
    x_ref, data_ref, w_ref, cos_ref, sin_ref, c_ref, s_ref, v_ref,
    o_ref,
    far_ref, got_ref, mis_ref, mu_ref, ma_ref, mat_ref, mbt_ref, g_ref, gr_ref, all_ref,
    send_f, recv_f, send_r, recv_r, send_m, recv_m, send_g, recv_g, send_o, recv_o,
):
    e = pl.program_id(0)
    blocks = pl.num_programs(0)
    groups, pair = ma_ref.shape[:2]
    half = pair // 2
    lanes = groups * pair
    nb, _, sub, tb = c_ref.shape
    me = lax.axis_index("dir")
    spot = lax.axis_index("elem")

    @pl.when(e == 0)
    def _():
        meet("dir", "elem")
        first = COS[-1] * mm(x_ref[...], cos_ref[...])
        second = SIN[-1] * mm(x_ref[...], sin_ref[...])
        far = jnp.concatenate(
            [first[:half] + second[half:], first[half:] - second[:half]], axis=0
        )
        wide = far_ref.shape[2]
        for k in range(far_ref.shape[0]):
            far_ref[k] = far[:, k * wide : (k + 1) * wide]
        got_ref[spot] = far_ref[spot]
        for peer in peers_of("elem"):
            push(
                far_ref.at[peer], got_ref.at[spot],
                send_f.at[peer], recv_f.at[spot], "elem", peer,
            ).start()
        for peer in peers_of("elem"):
            done = push(
                far_ref.at[peer], got_ref.at[peer],
                send_f.at[peer], recv_f.at[peer], "elem", peer,
            )
            done.wait_send()
            done.wait_recv()
        mis_ref[spot] = (jnp.sum(got_ref[...], axis=0) - data_ref[spot]).astype(bf16)
        for peer in peers_of("elem"):
            push(
                mis_ref.at[spot], mis_ref.at[spot],
                send_r.at[peer], recv_r.at[spot], "elem", peer,
            ).start()
        for peer in peers_of("elem"):
            done = push(
                mis_ref.at[spot], mis_ref.at[peer],
                send_r.at[peer], recv_r.at[peer], "elem", peer,
            )
            done.wait_send()
            done.wait_recv()
        res = jnp.concatenate([mis_ref[k] for k in range(mis_ref.shape[0])], axis=1)
        for j in range(nb):
            cols = slice(j * tb, (j + 1) * tb)
            first = COS[-1] * mt(res, cos_ref[cols, :])
            second = SIN[-1] * mt(res, sin_ref[cols, :])
            mu = jnp.concatenate(
                [first[:half] - second[half:], first[half:] + second[:half]], axis=0
            )
            mu_ref[:, cols] = (w_ref[:, cols] * mu).astype(bf16)
        ma_ref[me] = mu_ref[...]
        for peer in peers_of("dir"):
            push(mu_ref, ma_ref.at[me], send_m.at[peer], recv_m.at[me], "dir", peer).start()
        for peer in peers_of("dir"):
            done = push(
                mu_ref, ma_ref.at[peer], send_m.at[peer], recv_m.at[peer], "dir", peer
            )
            done.wait_send()
            done.wait_recv()
        for j in range(nb):
            cols = slice(j * tb, (j + 1) * tb)
            ma = ma_ref[:, :, cols].astype(f32)
            mb = jnp.concatenate([ma[:, half:], -ma[:, :half]], axis=1)
            mat_ref[j] = ma.reshape(lanes, tb).T.astype(bf16)
            mbt_ref[j] = mb.reshape(lanes, tb).T.astype(bf16)

    first = mm(c_ref[0, 0], mat_ref[0])
    second = mm(s_ref[0, 0], mbt_ref[0])
    for j in range(1, nb):
        first += mm(c_ref[j, 0], mat_ref[j])
        second += mm(s_ref[j, 0], mbt_ref[j])
    nu = ((TURNS * COS[-1]) * first + (TURNS * SIN[-1]) * second).T
    v = v_ref[0].reshape(lanes, sub).astype(f32)
    g_ref[e] = jnp.broadcast_to(jnp.sum(nu * v, axis=0, keepdims=True), (8, sub))

    @pl.when(e == blocks - 1)
    def _():
        gr_ref[spot] = g_ref[spot]
        for peer in peers_of("elem"):
            push(
                g_ref.at[peer], gr_ref.at[spot], send_g.at[peer], recv_g.at[spot], "elem", peer
            ).start()
        for peer in peers_of("elem"):
            done = push(
                g_ref.at[peer], gr_ref.at[peer], send_g.at[peer], recv_g.at[peer], "elem", peer
            )
            done.wait_send()
            done.wait_recv()
        all_ref[me] = jnp.sum(gr_ref[...], axis=0)
        for peer in peers_of("dir"):
            push(
                all_ref.at[me], all_ref.at[me], send_o.at[peer], recv_o.at[me], "dir", peer
            ).start()
        for peer in peers_of("dir"):
            done = push(
                all_ref.at[me], all_ref.at[peer], send_o.at[peer], recv_o.at[peer], "dir", peer
            )
            done.wait_send()
            done.wait_recv()
        o_ref[...] = all_ref[...]


def backward(x, data, w, cos_t, sin_t, cos_k, sin_k, v):
    nb, blocks, sub, tb = cos_k.shape
    groups, pair = v.shape[1:3]
    table = pl.BlockSpec((nb, 1, sub, tb), lambda e: (0, e, 0, 0))
    cells = cos_k.size
    return pl.pallas_call(
        backward_body,
        grid=(blocks,),
        in_specs=[VM, VM, VM, VM, VM, table, table, pl.BlockSpec((1, *v.shape[1:]), lambda e: (e, 0, 0, 0))],
        out_specs=VM,
        out_shape=jax.ShapeDtypeStruct((groups, 8, sub), f32),
        scratch_shapes=[
            pltpu.VMEM(data.shape, f32),
            pltpu.VMEM(data.shape, f32),
            pltpu.VMEM(data.shape, bf16),
            pltpu.VMEM(x.shape, bf16),
            pltpu.VMEM((groups, *x.shape), bf16),
            pltpu.VMEM((nb, tb, groups * pair), bf16),
            pltpu.VMEM((nb, tb, groups * pair), bf16),
            pltpu.VMEM((blocks, 8, sub), f32),
            pltpu.VMEM((blocks, 8, sub), f32),
            pltpu.VMEM((groups, 8, sub), f32),
            DMA((blocks,)),
            DMA((blocks,)),
            DMA((blocks,)),
            DMA((blocks,)),
            DMA((groups,)),
            DMA((groups,)),
            DMA((blocks,)),
            DMA((blocks,)),
            DMA((groups,)),
            DMA((groups,)),
        ],
        compiler_params=params(2),
        cost_estimate=pl.CostEstimate(
            flops=cells * 4 * groups * pair, bytes_accessed=4 * cells, transcendentals=0
        ),
        name="backward",
    )(x, data, w, cos_t, sin_t, cos_k, sin_k, v)


def table_body(rb, a_ref, b_ref, c_ref, s_ref):
    def body(k, carry):
        rows = pl.ds(pl.multiple_of(k * rb, rb), rb)
        t = mm(a_ref[rows, :], b_ref[...])
        for strip in strips(rb):
            r = fraction(t[strip])
            z = r * r
            part = pl.ds(pl.multiple_of(k * rb + strip.start, strip.stop - strip.start), strip.stop - strip.start)
            c_ref[part, :] = monic(COS, z).astype(bf16)
            s_ref[part, :] = (monic(SIN, z) * r).astype(bf16)
        return carry

    lax.fori_loop(0, a_ref.shape[0] // rb, body, 0)


def far_table(a, b):
    rows = a.shape[0]
    recv = b.shape[1]
    tb = chunk_of(recv, 256)
    rb = chunk_of(rows, 512)
    col = lambda n: pl.BlockSpec((n, tb), lambda i: (0, i))
    out = jax.ShapeDtypeStruct((rows, recv), bf16)
    cells = rows * recv
    return pl.pallas_call(
        lambda *refs: table_body(rb, *refs),
        grid=(recv // tb,),
        in_specs=[pl.BlockSpec(a.shape, lambda i: (0, 0)), col(32)],
        out_specs=[col(rows), col(rows)],
        out_shape=[out, out],
        compiler_params=pltpu.CompilerParams(vmem_limit_bytes=48 * 2**20),
        cost_estimate=pl.CostEstimate(flops=cells * 30, bytes_accessed=4 * cells, transcendentals=0),
        name="far_table",
    )(a, b)


def on_device(panel_angles, impedance, quad_count, receivers, farfield_data, warm_density):
    rows = impedance.shape[0]
    count_dir = farfield_data.shape[1]
    groups = lax.axis_size("dir")
    blocks = lax.axis_size("elem")
    ndir = count_dir * groups
    sub = rows // groups
    me = lax.axis_index("dir")

    w_loc = weights(quad_count)
    wz_loc = w_loc * impedance
    pos_loc = positions(panel_angles)
    turn_loc = pos_loc * TURNS

    src = lax.dynamic_slice_in_dim(turn_loc, me * sub, sub, 1)
    v = (wz_loc * warm_density).astype(bf16)
    v = jnp.transpose(v.reshape(2 * count_dir, groups, sub), (1, 0, 2))

    left, right = distance_rows(src, turn_loc)
    tb = chunk_of(rows, 256)
    right = jnp.transpose(right.reshape(right.shape[0], rows // tb, tb), (1, 0, 2))
    cos_k, sin_k, v_all, image = forward(left, right, v, blocks)
    image = image.reshape(2, count_dir, rows)

    dvec = lattice(me * count_dir + jnp.arange(count_dir, dtype=jnp.int32), ndir)
    state = plane(dvec, pos_loc) - image

    left, right = product_rows(turn_loc, lattice(receivers, RBANK))
    cos_t, sin_t = far_table(pad_rows(left).T, pad_rows(right))
    pair = 2 * count_dir
    recv = farfield_data.shape[2]
    data = jnp.transpose(farfield_data.reshape(pair, blocks, recv // blocks), (1, 0, 2))
    moved = (w_loc * state).astype(bf16).reshape(pair, rows)
    grad = backward(moved, data, w_loc[None], cos_t, sin_t, cos_k, sin_k, v_all)
    return (grad[:, 0].reshape(rows) / (-ndir * wz_loc), state)


def solution(mesh):
    placed = (
        P(None, "elem"),
        P("elem"),
        P("elem"),
        P(),
        P(None, "dir", None),
        P(None, "dir", "elem"),
    )
    return jax.shard_map(
        on_device,
        mesh=mesh,
        in_specs=placed,
        out_specs=(P("elem"), P(None, "dir", "elem")),
        check_vma=False,
    )
```

```python
import math

import jax
import jax.numpy as jnp
from jax import lax
from jax.experimental import pallas as pl
from jax.experimental.pallas import tpu as pltpu
from jax.sharding import PartitionSpec as P

PANELS = 16384
RBANK = 4096

WAVENUM = 32.0
SOFTEN = 0.0025
TURNS = WAVENUM / (2.0 * math.pi)
MAGIC = 12582912.0

COS = (1.41420401, -6.97763732, 5.71518787, -1.72821389)
SIN = (4.44287957, -7.30781668, 3.59777418, -0.791199392)

f32 = jnp.float32
bf16 = jnp.bfloat16


def positions(angles):
    phi = angles[0]
    psi = angles[1]
    return jnp.stack(
        [4.0 * jnp.cos(psi), jnp.sin(psi) * jnp.cos(phi), 0.6 * jnp.sin(psi) * jnp.sin(phi)]
    )


def weights(counts):
    return counts.astype(f32) * (0.5 / (4.0 * math.sqrt(PANELS)))


def lattice(index, count):
    where = index.astype(f32)
    height = 1.0 - (2.0 * where + 1.0) / count
    radius = jnp.sqrt(1.0 - height * height)
    turn = where * (math.pi * (3.0 - math.sqrt(5.0)))
    return jnp.stack([radius * jnp.cos(turn), radius * jnp.sin(turn), height])


def plane(dvec, pos):
    phase = WAVENUM * jnp.sum(dvec[:, :, None] * pos[:, None, :], axis=0)
    return jnp.stack([jnp.cos(phase), jnp.sin(phase)])


def pieces(x):
    hi = lax.reduce_precision(x, 8, 7)
    mid = lax.reduce_precision(x - hi, 8, 7)
    return hi, mid, (x - hi) - mid


def product_rows(a, b):
    ah, am, al = pieces(a)
    bh, bm, bl = pieces(b)
    left = jnp.concatenate([ah, ah, am, am, ah, al], axis=0)
    right = jnp.concatenate([bh, bm, bh, bm, bl, bh], axis=0)
    return left, right


def pad_rows(x):
    return jnp.pad(x, ((0, 32 - x.shape[0]), (0, 0))).astype(bf16)


def distance_rows(src, tgt):
    left, right = product_rows(-2.0 * src, tgt)
    ones_s = jnp.ones((3, src.shape[1]), f32)
    ones_t = jnp.ones((3, tgt.shape[1]), f32)
    sq_s = jnp.stack(pieces(jnp.sum(src * src, axis=0)))
    sq_t = jnp.stack(pieces(jnp.sum(tgt * tgt, axis=0) + SOFTEN * TURNS * TURNS))
    left = jnp.concatenate([left, sq_s, ones_s], axis=0)
    right = jnp.concatenate([right, ones_t, sq_t], axis=0)
    return pad_rows(left), pad_rows(right)


def horner(coefs, z):
    total = coefs[-1] * z + coefs[-2]
    for c in coefs[-3::-1]:
        total = total * z + c
    return total


def half_turn(t):
    r = t - ((t + MAGIC) - MAGIC)
    z = r * r
    return horner(COS, z), horner(SIN, z) * r


def green(d2):
    inv = lax.rsqrt(d2)
    c, s = half_turn(d2 * inv)
    over = s * inv
    return (inv - s * over).astype(bf16), (c * over).astype(bf16)


def strips(rows):
    step = min(rows, 32)
    return [slice(i, i + step) for i in range(0, rows, step)]


def mm(a, b):
    return lax.dot_general(a, b, (((1,), (0,)), ((), ())), preferred_element_type=f32)


def mt(a, b):
    return lax.dot_general(a, b, (((1,), (1,)), ((), ())), preferred_element_type=f32)


def chunk_of(total, most):
    size = min(total, most)
    while total % size:
        size //= 2
    return size


def peers_of(name):
    me = lax.axis_index(name)
    size = lax.axis_size(name)
    return [lax.rem(me + step, size) for step in range(1, size)]


def meet(*names):
    barrier = pltpu.get_barrier_semaphore()
    total = 0
    for name in names:
        for peer in peers_of(name):
            pl.semaphore_signal(
                barrier, inc=1, device_id={name: peer}, device_id_type=pl.DeviceIdType.MESH
            )
            total += 1
    pl.semaphore_wait(barrier, total)


def push(src, dst, send, recv, name, peer):
    return pltpu.make_async_remote_copy(
        src_ref=src,
        dst_ref=dst,
        send_sem=send,
        recv_sem=recv,
        device_id={name: peer},
        device_id_type=pl.DeviceIdType.MESH,
    )


def params(collective_id):
    return pltpu.CompilerParams(
        collective_id=collective_id, has_side_effects=True, vmem_limit_bytes=56 * 2**20
    )


VM = pl.BlockSpec(memory_space=pltpu.VMEM)
HBM = pl.BlockSpec(memory_space=pl.ANY)
DMA = pltpu.SemaphoreType.DMA


def forward_body(
    a_ref, b_ref, v_ref,
    c_out, s_out, vg_ref, image_ref,
    c_ref, s_ref, geo_ref, at_ref, part_ref, vb_ref, u_ref, ur_ref,
    send_x, recv_x, send_a, recv_a, send_b, recv_b, send_u, recv_u, sem_c, sem_s,
):
    blocks, sub = at_ref.shape[:2]
    nb, _, tb = b_ref.shape
    groups, pair = v_ref.shape[:2]
    half = pair // 2
    lanes = groups * pair
    lag = max(1, (3 * nb) // 8)
    me = lax.axis_index("dir")
    spot = lax.axis_index("elem")

    def make(j, e):
        d2 = mm(at_ref[e], b_ref[j])
        for strip in strips(sub):
            cos_k, sin_k = green(d2[strip])
            c_ref[j, e, strip, :] = cos_k
            s_ref[j, e, strip, :] = sin_k

    def use(j, e):
        va = vg_ref[e].reshape(lanes, sub)
        vb = vb_ref[e].reshape(lanes, sub)
        total = TURNS * (mm(va, c_ref[j, e]) + mm(vb, s_ref[j, e]))
        u_ref[j] += total.reshape(groups, pair, tb)

    def start_out(j):
        pltpu.make_async_copy(c_ref.at[j], c_out.at[j], sem_c.at[j]).start()
        pltpu.make_async_copy(s_ref.at[j], s_out.at[j], sem_s.at[j]).start()

    def send_block(j):
        for peer in peers_of("dir"):
            push(
                u_ref.at[j, peer], ur_ref.at[me, j],
                send_u.at[peer, j], recv_u.at[me, j], "dir", peer,
            ).start()

    def others(act):
        at = lambda i: lax.rem(spot + i, blocks)

        def two(i, c):
            act([at(2 * i + 1), at(2 * i + 2)])
            return c

        pairs = (blocks - 1) // 2
        lax.fori_loop(0, pairs, two, 0)
        if blocks - 1 > 2 * pairs:
            act([at(blocks - 1)])

    def make_only(j, carry):
        others(lambda es: [make(j, e) for e in es])
        start_out(j)
        return carry

    def both(j, carry):
        others(lambda es: [use(j - lag, e) for e in es] + [make(j, e) for e in es])
        use(j - lag, spot)
        start_out(j)
        send_block(j - lag)
        return carry

    def use_only(j, carry):
        lax.fori_loop(0, blocks, lambda e, c: (use(j, e), c)[1], 0)
        send_block(j)
        return carry

    part_ref[me] = v_ref[me]
    geo_ref[spot] = a_ref[...]
    meet("dir", "elem")
    for peer in peers_of("elem"):
        push(
            a_ref, geo_ref.at[spot], send_x.at[peer], recv_x.at[spot], "elem", peer
        ).start()
    for peer in peers_of("dir"):
        push(
            v_ref.at[peer], part_ref.at[me], send_a.at[peer], recv_a.at[me], "dir", peer
        ).start()
    u_ref[...] = jnp.zeros_like(u_ref)
    at_ref[spot] = a_ref[...].astype(f32).T.astype(bf16)

    def make_own(j, carry):
        make(j, spot)
        return carry

    lax.fori_loop(0, nb, make_own, 0)
    for peer in peers_of("dir"):
        done = push(
            v_ref.at[peer], part_ref.at[peer], send_a.at[peer], recv_a.at[peer], "dir", peer
        )
        done.wait_send()
        done.wait_recv()
    vg_ref[spot] = part_ref[...]
    for peer in peers_of("elem"):
        push(
            part_ref, vg_ref.at[spot], send_b.at[peer], recv_b.at[spot], "elem", peer
        ).start()
    for peer in peers_of("elem"):
        done = push(a_ref, geo_ref.at[peer], send_x.at[peer], recv_x.at[peer], "elem", peer)
        done.wait_send()
        done.wait_recv()
    for e in range(blocks):
        at_ref[e] = geo_ref[e].astype(f32).T.astype(bf16)
    lax.fori_loop(0, lag, make_only, 0)
    for peer in peers_of("elem"):
        done = push(
            part_ref, vg_ref.at[peer], send_b.at[peer], recv_b.at[peer], "elem", peer
        )
        done.wait_send()
        done.wait_recv()
    vb_ref[:, :, :half] = -vg_ref[:, :, half:]
    vb_ref[:, :, half:] = vg_ref[:, :, :half]

    lax.fori_loop(lag, nb, both, 0)
    lax.fori_loop(nb - lag, nb, use_only, 0)

    for j in range(nb):
        total = u_ref[j, me]
        for peer in peers_of("dir"):
            done = push(
                u_ref.at[j, peer], ur_ref.at[peer, j],
                send_u.at[peer, j], recv_u.at[peer, j], "dir", peer,
            )
            done.wait_send()
            done.wait_recv()
            total += ur_ref[peer, j]
        image_ref[:, j * tb : (j + 1) * tb] = total
    for j in range(nb):
        pltpu.make_async_copy(c_ref.at[j], c_out.at[j], sem_c.at[j]).wait()
        pltpu.make_async_copy(s_ref.at[j], s_out.at[j], sem_s.at[j]).wait()


def forward(a, b, v, blocks):
    sub = a.shape[1]
    nb, _, tb = b.shape
    groups, pair = v.shape[:2]
    table = (nb, blocks, sub, tb)
    cells = nb * blocks * sub * tb
    return pl.pallas_call(
        forward_body,
        in_specs=[VM, VM, VM],
        out_specs=[HBM, HBM, VM, VM],
        out_shape=[
            jax.ShapeDtypeStruct(table, bf16),
            jax.ShapeDtypeStruct(table, bf16),
            jax.ShapeDtypeStruct((blocks, groups, pair, sub), bf16),
            jax.ShapeDtypeStruct((pair, nb * tb), f32),
        ],
        scratch_shapes=[
            pltpu.VMEM(table, bf16),
            pltpu.VMEM(table, bf16),
            pltpu.VMEM((blocks, *a.shape), bf16),
            pltpu.VMEM((blocks, sub, a.shape[0]), bf16),
            pltpu.VMEM((groups, pair, sub), bf16),
            pltpu.VMEM((blocks, groups, pair, sub), bf16),
            pltpu.VMEM((nb, groups, pair, tb), f32),
            pltpu.VMEM((groups, nb, pair, tb), f32),
            DMA((blocks,)),
            DMA((blocks,)),
            DMA((groups,)),
            DMA((groups,)),
            DMA((blocks,)),
            DMA((blocks,)),
            DMA((groups, nb)),
            DMA((groups, nb)),
            DMA((nb,)),
            DMA((nb,)),
        ],
        compiler_params=params(1),
        cost_estimate=pl.CostEstimate(
            flops=cells * 4 * groups * pair, bytes_accessed=4 * cells, transcendentals=cells
        ),
        name="forward",
    )(a, b, v)


def backward_body(
    x_ref, data_ref, w_ref, cos_ref, sin_ref, c_ref, s_ref, v_ref,
    o_ref,
    far_ref, got_ref, mis_ref, mu_ref, ma_ref, mat_ref, mbt_ref, g_ref, gr_ref, all_ref,
    send_f, recv_f, send_r, recv_r, send_m, recv_m, send_g, recv_g, send_o, recv_o,
):
    e = pl.program_id(0)
    blocks = pl.num_programs(0)
    groups, pair = ma_ref.shape[:2]
    half = pair // 2
    lanes = groups * pair
    nb, _, sub, tb = c_ref.shape
    me = lax.axis_index("dir")
    spot = lax.axis_index("elem")

    @pl.when(e == 0)
    def _():
        meet("dir", "elem")
        first = mm(x_ref[...], cos_ref[...])
        second = mm(x_ref[...], sin_ref[...])
        far = jnp.concatenate(
            [first[:half] + second[half:], first[half:] - second[:half]], axis=0
        )
        wide = far_ref.shape[2]
        for k in range(far_ref.shape[0]):
            far_ref[k] = far[:, k * wide : (k + 1) * wide]
        got_ref[spot] = far_ref[spot]
        for peer in peers_of("elem"):
            push(
                far_ref.at[peer], got_ref.at[spot],
                send_f.at[peer], recv_f.at[spot], "elem", peer,
            ).start()
        for peer in peers_of("elem"):
            done = push(
                far_ref.at[peer], got_ref.at[peer],
                send_f.at[peer], recv_f.at[peer], "elem", peer,
            )
            done.wait_send()
            done.wait_recv()
        mis_ref[spot] = (jnp.sum(got_ref[...], axis=0) - data_ref[spot]).astype(bf16)
        for peer in peers_of("elem"):
            push(
                mis_ref.at[spot], mis_ref.at[spot],
                send_r.at[peer], recv_r.at[spot], "elem", peer,
            ).start()
        for peer in peers_of("elem"):
            done = push(
                mis_ref.at[spot], mis_ref.at[peer],
                send_r.at[peer], recv_r.at[peer], "elem", peer,
            )
            done.wait_send()
            done.wait_recv()
        res = jnp.concatenate([mis_ref[k] for k in range(mis_ref.shape[0])], axis=1)
        for j in range(nb):
            cols = slice(j * tb, (j + 1) * tb)
            first = mt(res, cos_ref[cols, :])
            second = mt(res, sin_ref[cols, :])
            mu = jnp.concatenate(
                [first[:half] - second[half:], first[half:] + second[:half]], axis=0
            )
            mu_ref[:, cols] = (w_ref[:, cols] * mu).astype(bf16)
        ma_ref[me] = mu_ref[...]
        for peer in peers_of("dir"):
            push(mu_ref, ma_ref.at[me], send_m.at[peer], recv_m.at[me], "dir", peer).start()
        for peer in peers_of("dir"):
            done = push(
                mu_ref, ma_ref.at[peer], send_m.at[peer], recv_m.at[peer], "dir", peer
            )
            done.wait_send()
            done.wait_recv()
        for j in range(nb):
            cols = slice(j * tb, (j + 1) * tb)
            ma = ma_ref[:, :, cols].astype(f32)
            mb = jnp.concatenate([ma[:, half:], -ma[:, :half]], axis=1)
            mat_ref[j] = ma.reshape(lanes, tb).T.astype(bf16)
            mbt_ref[j] = mb.reshape(lanes, tb).T.astype(bf16)

    first = mm(c_ref[0, 0], mat_ref[0])
    second = mm(s_ref[0, 0], mbt_ref[0])
    for j in range(1, nb):
        first += mm(c_ref[j, 0], mat_ref[j])
        second += mm(s_ref[j, 0], mbt_ref[j])
    nu = (TURNS * (first + second)).T
    v = v_ref[0].reshape(lanes, sub).astype(f32)
    g_ref[e] = jnp.broadcast_to(jnp.sum(nu * v, axis=0, keepdims=True), (8, sub))

    @pl.when(e == blocks - 1)
    def _():
        gr_ref[spot] = g_ref[spot]
        for peer in peers_of("elem"):
            push(
                g_ref.at[peer], gr_ref.at[spot], send_g.at[peer], recv_g.at[spot], "elem", peer
            ).start()
        for peer in peers_of("elem"):
            done = push(
                g_ref.at[peer], gr_ref.at[peer], send_g.at[peer], recv_g.at[peer], "elem", peer
            )
            done.wait_send()
            done.wait_recv()
        all_ref[me] = jnp.sum(gr_ref[...], axis=0)
        for peer in peers_of("dir"):
            push(
                all_ref.at[me], all_ref.at[me], send_o.at[peer], recv_o.at[me], "dir", peer
            ).start()
        for peer in peers_of("dir"):
            done = push(
                all_ref.at[me], all_ref.at[peer], send_o.at[peer], recv_o.at[peer], "dir", peer
            )
            done.wait_send()
            done.wait_recv()
        o_ref[...] = all_ref[...]


def backward(x, data, w, cos_t, sin_t, cos_k, sin_k, v):
    nb, blocks, sub, tb = cos_k.shape
    groups, pair = v.shape[1:3]
    table = pl.BlockSpec((nb, 1, sub, tb), lambda e: (0, e, 0, 0))
    cells = cos_k.size
    return pl.pallas_call(
        backward_body,
        grid=(blocks,),
        in_specs=[VM, VM, VM, VM, VM, table, table, pl.BlockSpec((1, *v.shape[1:]), lambda e: (e, 0, 0, 0))],
        out_specs=VM,
        out_shape=jax.ShapeDtypeStruct((groups, 8, sub), f32),
        scratch_shapes=[
            pltpu.VMEM(data.shape, f32),
            pltpu.VMEM(data.shape, f32),
            pltpu.VMEM(data.shape, bf16),
            pltpu.VMEM(x.shape, bf16),
            pltpu.VMEM((groups, *x.shape), bf16),
            pltpu.VMEM((nb, tb, groups * pair), bf16),
            pltpu.VMEM((nb, tb, groups * pair), bf16),
            pltpu.VMEM((blocks, 8, sub), f32),
            pltpu.VMEM((blocks, 8, sub), f32),
            pltpu.VMEM((groups, 8, sub), f32),
            DMA((blocks,)),
            DMA((blocks,)),
            DMA((blocks,)),
            DMA((blocks,)),
            DMA((groups,)),
            DMA((groups,)),
            DMA((blocks,)),
            DMA((blocks,)),
            DMA((groups,)),
            DMA((groups,)),
        ],
        compiler_params=params(2),
        cost_estimate=pl.CostEstimate(
            flops=cells * 4 * groups * pair, bytes_accessed=4 * cells, transcendentals=0
        ),
        name="backward",
    )(x, data, w, cos_t, sin_t, cos_k, sin_k, v)


def table_body(rb, a_ref, b_ref, c_ref, s_ref):
    def body(k, carry):
        rows = pl.ds(pl.multiple_of(k * rb, rb), rb)
        t = mm(a_ref[rows, :], b_ref[...])
        for strip in strips(rb):
            cos_h, sin_h = half_turn(t[strip])
            part = pl.ds(pl.multiple_of(k * rb + strip.start, strip.stop - strip.start), strip.stop - strip.start)
            c_ref[part, :] = (1.0 - sin_h * sin_h).astype(bf16)
            s_ref[part, :] = (cos_h * sin_h).astype(bf16)
        return carry

    lax.fori_loop(0, a_ref.shape[0] // rb, body, 0)


def far_table(a, b):
    rows = a.shape[0]
    recv = b.shape[1]
    tb = chunk_of(recv, 256)
    rb = chunk_of(rows, 1024)
    col = lambda n: pl.BlockSpec((n, tb), lambda i: (0, i))
    out = jax.ShapeDtypeStruct((rows, recv), bf16)
    cells = rows * recv
    return pl.pallas_call(
        lambda *refs: table_body(rb, *refs),
        grid=(recv // tb,),
        in_specs=[pl.BlockSpec(a.shape, lambda i: (0, 0)), col(32)],
        out_specs=[col(rows), col(rows)],
        out_shape=[out, out],
        compiler_params=pltpu.CompilerParams(vmem_limit_bytes=48 * 2**20),
        cost_estimate=pl.CostEstimate(flops=cells * 30, bytes_accessed=4 * cells, transcendentals=0),
        name="far_table",
    )(a, b)


def on_device(panel_angles, impedance, quad_count, receivers, farfield_data, warm_density):
    rows = impedance.shape[0]
    count_dir = farfield_data.shape[1]
    groups = lax.axis_size("dir")
    blocks = lax.axis_size("elem")
    ndir = count_dir * groups
    sub = rows // groups
    me = lax.axis_index("dir")

    w_loc = weights(quad_count)
    wz_loc = w_loc * impedance
    pos_loc = positions(panel_angles)
    turn_loc = pos_loc * TURNS

    src = lax.dynamic_slice_in_dim(turn_loc, me * sub, sub, 1)
    v = (wz_loc * warm_density).astype(bf16)
    v = jnp.transpose(v.reshape(2 * count_dir, groups, sub), (1, 0, 2))

    left, right = distance_rows(src, turn_loc)
    tb = chunk_of(rows, 256)
    right = jnp.transpose(right.reshape(right.shape[0], rows // tb, tb), (1, 0, 2))
    cos_k, sin_k, v_all, image = forward(left, right, v, blocks)
    image = image.reshape(2, count_dir, rows)

    dvec = lattice(me * count_dir + jnp.arange(count_dir, dtype=jnp.int32), ndir)
    state = plane(dvec, pos_loc) - image

    left, right = product_rows(turn_loc, lattice(receivers, RBANK))
    cos_t, sin_t = far_table(pad_rows(left).T, pad_rows(right))
    pair = 2 * count_dir
    recv = farfield_data.shape[2]
    data = jnp.transpose(farfield_data.reshape(pair, blocks, recv // blocks), (1, 0, 2))
    moved = (w_loc * state).astype(bf16).reshape(pair, rows)
    grad = backward(moved, data, w_loc[None], cos_t, sin_t, cos_k, sin_k, v_all)
    return (grad[:, 0].reshape(rows) / (-ndir * wz_loc), state)


def solution(mesh):
    placed = (
        P(None, "elem"),
        P("elem"),
        P("elem"),
        P(),
        P(None, "dir", None),
        P(None, "dir", "elem"),
    )
    return jax.shard_map(
        on_device,
        mesh=mesh,
        in_specs=placed,
        out_specs=(P("elem"), P(None, "dir", "elem")),
        check_vma=False,
    )
```

```python
import math

import jax
import jax.numpy as jnp
from jax import lax
from jax.experimental import pallas as pl
from jax.experimental.pallas import tpu as pltpu
from jax.sharding import PartitionSpec as P

PANELS = 16384
RBANK = 4096

WAVENUM = 32.0
SOFTEN = 0.0025
TURNS = WAVENUM / (2.0 * math.pi)
MAGIC = 12582912.0

COS = (1.41420401, -6.97763732, 5.71518787, -1.72821389)
SIN = (4.44287957, -7.30781668, 3.59777418, -0.791199392)

f32 = jnp.float32
bf16 = jnp.bfloat16


def positions(angles):
    phi = angles[0]
    psi = angles[1]
    return jnp.stack(
        [4.0 * jnp.cos(psi), jnp.sin(psi) * jnp.cos(phi), 0.6 * jnp.sin(psi) * jnp.sin(phi)]
    )


def weights(counts):
    return counts.astype(f32) * (0.5 / (4.0 * math.sqrt(PANELS)))


def lattice(index, count):
    where = index.astype(f32)
    height = 1.0 - (2.0 * where + 1.0) / count
    radius = jnp.sqrt(1.0 - height * height)
    turn = where * (math.pi * (3.0 - math.sqrt(5.0)))
    return jnp.stack([radius * jnp.cos(turn), radius * jnp.sin(turn), height])


def plane(dvec, pos):
    phase = WAVENUM * jnp.sum(dvec[:, :, None] * pos[:, None, :], axis=0)
    return jnp.stack([jnp.cos(phase), jnp.sin(phase)])


def pieces(x):
    hi = lax.reduce_precision(x, 8, 7)
    mid = lax.reduce_precision(x - hi, 8, 7)
    return hi, mid, (x - hi) - mid


def product_rows(a, b):
    ah, am, al = pieces(a)
    bh, bm, bl = pieces(b)
    left = jnp.concatenate([ah, ah, am, am, ah, al], axis=0)
    right = jnp.concatenate([bh, bm, bh, bm, bl, bh], axis=0)
    return left, right


def pad_rows(x):
    return jnp.pad(x, ((0, 32 - x.shape[0]), (0, 0))).astype(bf16)


def distance_rows(src, tgt):
    left, right = product_rows(-2.0 * src, tgt)
    ones_s = jnp.ones((3, src.shape[1]), f32)
    ones_t = jnp.ones((3, tgt.shape[1]), f32)
    sq_s = jnp.stack(pieces(jnp.sum(src * src, axis=0)))
    sq_t = jnp.stack(pieces(jnp.sum(tgt * tgt, axis=0) + SOFTEN * TURNS * TURNS))
    left = jnp.concatenate([left, sq_s, ones_s], axis=0)
    right = jnp.concatenate([right, ones_t, sq_t], axis=0)
    return pad_rows(left), pad_rows(right)


def horner(coefs, z):
    total = coefs[-1] * z + coefs[-2]
    for c in coefs[-3::-1]:
        total = total * z + c
    return total


def half_turn(t):
    r = t - ((t + MAGIC) - MAGIC)
    z = r * r
    return horner(COS, z), horner(SIN, z) * r


def green(d2):
    inv = lax.rsqrt(d2)
    c, s = half_turn(d2 * inv)
    over = s * inv
    return (inv - s * over).astype(bf16), (c * over).astype(bf16)


def strips(rows):
    step = min(rows, 32)
    return [slice(i, i + step) for i in range(0, rows, step)]


def mm(a, b):
    return lax.dot_general(a, b, (((1,), (0,)), ((), ())), preferred_element_type=f32)


def mt(a, b):
    return lax.dot_general(a, b, (((1,), (1,)), ((), ())), preferred_element_type=f32)


def chunk_of(total, most):
    size = min(total, most)
    while total % size:
        size //= 2
    return size


def peers_of(name):
    me = lax.axis_index(name)
    size = lax.axis_size(name)
    return [lax.rem(me + step, size) for step in range(1, size)]


def meet(*names):
    barrier = pltpu.get_barrier_semaphore()
    total = 0
    for name in names:
        for peer in peers_of(name):
            pl.semaphore_signal(
                barrier, inc=1, device_id={name: peer}, device_id_type=pl.DeviceIdType.MESH
            )
            total += 1
    pl.semaphore_wait(barrier, total)


def push(src, dst, send, recv, name, peer):
    return pltpu.make_async_remote_copy(
        src_ref=src,
        dst_ref=dst,
        send_sem=send,
        recv_sem=recv,
        device_id={name: peer},
        device_id_type=pl.DeviceIdType.MESH,
    )


def params(collective_id):
    return pltpu.CompilerParams(
        collective_id=collective_id, has_side_effects=True, vmem_limit_bytes=56 * 2**20
    )


VM = pl.BlockSpec(memory_space=pltpu.VMEM)
HBM = pl.BlockSpec(memory_space=pl.ANY)
DMA = pltpu.SemaphoreType.DMA


def forward_body(
    a_ref, b_ref, v_ref,
    c_out, s_out, vg_ref, image_ref,
    c_ref, s_ref, geo_ref, at_ref, part_ref, vb_ref, u_ref, ur_ref,
    send_x, recv_x, send_a, recv_a, send_b, recv_b, send_u, recv_u, sem_c, sem_s,
):
    blocks, sub = at_ref.shape[:2]
    nb, _, tb = b_ref.shape
    groups, pair = v_ref.shape[:2]
    half = pair // 2
    lanes = groups * pair
    lag = max(1, nb // 4)
    me = lax.axis_index("dir")
    spot = lax.axis_index("elem")

    def make(j, e):
        d2 = mm(at_ref[e], b_ref[j])
        for strip in strips(sub):
            cos_k, sin_k = green(d2[strip])
            c_ref[j, e, strip, :] = cos_k
            s_ref[j, e, strip, :] = sin_k

    def use(j, e):
        va = vg_ref[e].reshape(lanes, sub)
        vb = vb_ref[e].reshape(lanes, sub)
        total = TURNS * (mm(va, c_ref[j, e]) + mm(vb, s_ref[j, e]))
        u_ref[j] += total.reshape(groups, pair, tb)

    def start_out(j):
        pltpu.make_async_copy(c_ref.at[j], c_out.at[j], sem_c.at[j]).start()
        pltpu.make_async_copy(s_ref.at[j], s_out.at[j], sem_s.at[j]).start()

    def send_block(j):
        for peer in peers_of("dir"):
            push(
                u_ref.at[j, peer], ur_ref.at[me, j],
                send_u.at[peer, j], recv_u.at[me, j], "dir", peer,
            ).start()

    def others(act):
        at = lambda i: lax.rem(spot + i, blocks)

        def two(i, c):
            act([at(2 * i + 1), at(2 * i + 2)])
            return c

        pairs = (blocks - 1) // 2
        lax.fori_loop(0, pairs, two, 0)
        if blocks - 1 > 2 * pairs:
            act([at(blocks - 1)])

    def make_only(j, carry):
        others(lambda es: [make(j, e) for e in es])
        start_out(j)
        return carry

    def both(j, carry):
        others(lambda es: [use(j - lag, e) for e in es] + [make(j, e) for e in es])
        use(j - lag, spot)
        start_out(j)
        send_block(j - lag)
        return carry

    def use_only(j, carry):
        lax.fori_loop(0, blocks, lambda e, c: (use(j, e), c)[1], 0)
        send_block(j)
        return carry

    part_ref[me] = v_ref[me]
    geo_ref[spot] = a_ref[...]
    meet("dir", "elem")
    for peer in peers_of("elem"):
        push(
            a_ref, geo_ref.at[spot], send_x.at[peer], recv_x.at[spot], "elem", peer
        ).start()
    for peer in peers_of("dir"):
        push(
            v_ref.at[peer], part_ref.at[me], send_a.at[peer], recv_a.at[me], "dir", peer
        ).start()
    u_ref[...] = jnp.zeros_like(u_ref)
    at_ref[spot] = a_ref[...].astype(f32).T.astype(bf16)

    def make_own(j, carry):
        make(j, spot)
        return carry

    lax.fori_loop(0, nb, make_own, 0)
    for peer in peers_of("dir"):
        done = push(
            v_ref.at[peer], part_ref.at[peer], send_a.at[peer], recv_a.at[peer], "dir", peer
        )
        done.wait_send()
        done.wait_recv()
    vg_ref[spot] = part_ref[...]
    for peer in peers_of("elem"):
        push(
            part_ref, vg_ref.at[spot], send_b.at[peer], recv_b.at[spot], "elem", peer
        ).start()
    for peer in peers_of("elem"):
        done = push(a_ref, geo_ref.at[peer], send_x.at[peer], recv_x.at[peer], "elem", peer)
        done.wait_send()
        done.wait_recv()
    for e in range(blocks):
        at_ref[e] = geo_ref[e].astype(f32).T.astype(bf16)
    lax.fori_loop(0, lag, make_only, 0)
    for peer in peers_of("elem"):
        done = push(
            part_ref, vg_ref.at[peer], send_b.at[peer], recv_b.at[peer], "elem", peer
        )
        done.wait_send()
        done.wait_recv()
    vb_ref[:, :, :half] = -vg_ref[:, :, half:]
    vb_ref[:, :, half:] = vg_ref[:, :, :half]

    lax.fori_loop(lag, nb, both, 0)
    lax.fori_loop(nb - lag, nb, use_only, 0)

    for j in range(nb):
        total = u_ref[j, me]
        for peer in peers_of("dir"):
            done = push(
                u_ref.at[j, peer], ur_ref.at[peer, j],
                send_u.at[peer, j], recv_u.at[peer, j], "dir", peer,
            )
            done.wait_send()
            done.wait_recv()
            total += ur_ref[peer, j]
        image_ref[:, j * tb : (j + 1) * tb] = total
    for j in range(nb):
        pltpu.make_async_copy(c_ref.at[j], c_out.at[j], sem_c.at[j]).wait()
        pltpu.make_async_copy(s_ref.at[j], s_out.at[j], sem_s.at[j]).wait()


def forward(a, b, v, blocks):
    sub = a.shape[1]
    nb, _, tb = b.shape
    groups, pair = v.shape[:2]
    table = (nb, blocks, sub, tb)
    cells = nb * blocks * sub * tb
    return pl.pallas_call(
        forward_body,
        in_specs=[VM, VM, VM],
        out_specs=[HBM, HBM, VM, VM],
        out_shape=[
            jax.ShapeDtypeStruct(table, bf16),
            jax.ShapeDtypeStruct(table, bf16),
            jax.ShapeDtypeStruct((blocks, groups, pair, sub), bf16),
            jax.ShapeDtypeStruct((pair, nb * tb), f32),
        ],
        scratch_shapes=[
            pltpu.VMEM(table, bf16),
            pltpu.VMEM(table, bf16),
            pltpu.VMEM((blocks, *a.shape), bf16),
            pltpu.VMEM((blocks, sub, a.shape[0]), bf16),
            pltpu.VMEM((groups, pair, sub), bf16),
            pltpu.VMEM((blocks, groups, pair, sub), bf16),
            pltpu.VMEM((nb, groups, pair, tb), f32),
            pltpu.VMEM((groups, nb, pair, tb), f32),
            DMA((blocks,)),
            DMA((blocks,)),
            DMA((groups,)),
            DMA((groups,)),
            DMA((blocks,)),
            DMA((blocks,)),
            DMA((groups, nb)),
            DMA((groups, nb)),
            DMA((nb,)),
            DMA((nb,)),
        ],
        compiler_params=params(1),
        cost_estimate=pl.CostEstimate(
            flops=cells * 4 * groups * pair, bytes_accessed=4 * cells, transcendentals=cells
        ),
        name="forward",
    )(a, b, v)


def backward_body(
    x_ref, data_ref, w_ref, cos_ref, sin_ref, c_ref, s_ref, v_ref,
    o_ref,
    far_ref, got_ref, mis_ref, mu_ref, ma_ref, mat_ref, mbt_ref, g_ref, gr_ref, all_ref,
    send_f, recv_f, send_r, recv_r, send_m, recv_m, send_g, recv_g, send_o, recv_o,
):
    e = pl.program_id(0)
    blocks = pl.num_programs(0)
    groups, pair = ma_ref.shape[:2]
    half = pair // 2
    lanes = groups * pair
    nb, _, sub, tb = c_ref.shape
    me = lax.axis_index("dir")
    spot = lax.axis_index("elem")

    @pl.when(e == 0)
    def _():
        meet("dir", "elem")
        first = mm(x_ref[...], cos_ref[...])
        second = mm(x_ref[...], sin_ref[...])
        far = jnp.concatenate(
            [first[:half] + second[half:], first[half:] - second[:half]], axis=0
        )
        wide = far_ref.shape[2]
        for k in range(far_ref.shape[0]):
            far_ref[k] = far[:, k * wide : (k + 1) * wide]
        got_ref[spot] = far_ref[spot]
        for peer in peers_of("elem"):
            push(
                far_ref.at[peer], got_ref.at[spot],
                send_f.at[peer], recv_f.at[spot], "elem", peer,
            ).start()
        for peer in peers_of("elem"):
            done = push(
                far_ref.at[peer], got_ref.at[peer],
                send_f.at[peer], recv_f.at[peer], "elem", peer,
            )
            done.wait_send()
            done.wait_recv()
        mis_ref[spot] = (jnp.sum(got_ref[...], axis=0) - data_ref[spot]).astype(bf16)
        for peer in peers_of("elem"):
            push(
                mis_ref.at[spot], mis_ref.at[spot],
                send_r.at[peer], recv_r.at[spot], "elem", peer,
            ).start()
        for peer in peers_of("elem"):
            done = push(
                mis_ref.at[spot], mis_ref.at[peer],
                send_r.at[peer], recv_r.at[peer], "elem", peer,
            )
            done.wait_send()
            done.wait_recv()
        res = jnp.concatenate([mis_ref[k] for k in range(mis_ref.shape[0])], axis=1)
        for j in range(nb):
            cols = slice(j * tb, (j + 1) * tb)
            first = mt(res, cos_ref[cols, :])
            second = mt(res, sin_ref[cols, :])
            mu = jnp.concatenate(
                [first[:half] - second[half:], first[half:] + second[:half]], axis=0
            )
            mu_ref[:, cols] = (w_ref[:, cols] * mu).astype(bf16)
        ma_ref[me] = mu_ref[...]
        for peer in peers_of("dir"):
            push(mu_ref, ma_ref.at[me], send_m.at[peer], recv_m.at[me], "dir", peer).start()
        for peer in peers_of("dir"):
            done = push(
                mu_ref, ma_ref.at[peer], send_m.at[peer], recv_m.at[peer], "dir", peer
            )
            done.wait_send()
            done.wait_recv()
        for j in range(nb):
            cols = slice(j * tb, (j + 1) * tb)
            ma = ma_ref[:, :, cols].astype(f32)
            mb = jnp.concatenate([ma[:, half:], -ma[:, :half]], axis=1)
            mat_ref[j] = ma.reshape(lanes, tb).T.astype(bf16)
            mbt_ref[j] = mb.reshape(lanes, tb).T.astype(bf16)

    first = mm(c_ref[0, 0], mat_ref[0])
    second = mm(s_ref[0, 0], mbt_ref[0])
    for j in range(1, nb):
        first += mm(c_ref[j, 0], mat_ref[j])
        second += mm(s_ref[j, 0], mbt_ref[j])
    nu = (TURNS * (first + second)).T
    v = v_ref[0].reshape(lanes, sub).astype(f32)
    g_ref[e] = jnp.broadcast_to(jnp.sum(nu * v, axis=0, keepdims=True), (8, sub))

    @pl.when(e == blocks - 1)
    def _():
        gr_ref[spot] = g_ref[spot]
        for peer in peers_of("elem"):
            push(
                g_ref.at[peer], gr_ref.at[spot], send_g.at[peer], recv_g.at[spot], "elem", peer
            ).start()
        for peer in peers_of("elem"):
            done = push(
                g_ref.at[peer], gr_ref.at[peer], send_g.at[peer], recv_g.at[peer], "elem", peer
            )
            done.wait_send()
            done.wait_recv()
        all_ref[me] = jnp.sum(gr_ref[...], axis=0)
        for peer in peers_of("dir"):
            push(
                all_ref.at[me], all_ref.at[me], send_o.at[peer], recv_o.at[me], "dir", peer
            ).start()
        for peer in peers_of("dir"):
            done = push(
                all_ref.at[me], all_ref.at[peer], send_o.at[peer], recv_o.at[peer], "dir", peer
            )
            done.wait_send()
            done.wait_recv()
        o_ref[...] = all_ref[...]


def backward(x, data, w, cos_t, sin_t, cos_k, sin_k, v):
    nb, blocks, sub, tb = cos_k.shape
    groups, pair = v.shape[1:3]
    table = pl.BlockSpec((nb, 1, sub, tb), lambda e: (0, e, 0, 0))
    cells = cos_k.size
    return pl.pallas_call(
        backward_body,
        grid=(blocks,),
        in_specs=[VM, VM, VM, VM, VM, table, table, pl.BlockSpec((1, *v.shape[1:]), lambda e: (e, 0, 0, 0))],
        out_specs=VM,
        out_shape=jax.ShapeDtypeStruct((groups, 8, sub), f32),
        scratch_shapes=[
            pltpu.VMEM(data.shape, f32),
            pltpu.VMEM(data.shape, f32),
            pltpu.VMEM(data.shape, bf16),
            pltpu.VMEM(x.shape, bf16),
            pltpu.VMEM((groups, *x.shape), bf16),
            pltpu.VMEM((nb, tb, groups * pair), bf16),
            pltpu.VMEM((nb, tb, groups * pair), bf16),
            pltpu.VMEM((blocks, 8, sub), f32),
            pltpu.VMEM((blocks, 8, sub), f32),
            pltpu.VMEM((groups, 8, sub), f32),
            DMA((blocks,)),
            DMA((blocks,)),
            DMA((blocks,)),
            DMA((blocks,)),
            DMA((groups,)),
            DMA((groups,)),
            DMA((blocks,)),
            DMA((blocks,)),
            DMA((groups,)),
            DMA((groups,)),
        ],
        compiler_params=params(2),
        cost_estimate=pl.CostEstimate(
            flops=cells * 4 * groups * pair, bytes_accessed=4 * cells, transcendentals=0
        ),
        name="backward",
    )(x, data, w, cos_t, sin_t, cos_k, sin_k, v)


def table_body(rb, a_ref, b_ref, c_ref, s_ref):
    def body(k, carry):
        rows = pl.ds(pl.multiple_of(k * rb, rb), rb)
        t = mm(a_ref[rows, :], b_ref[...])
        for strip in strips(rb):
            cos_h, sin_h = half_turn(t[strip])
            part = pl.ds(pl.multiple_of(k * rb + strip.start, strip.stop - strip.start), strip.stop - strip.start)
            c_ref[part, :] = (1.0 - sin_h * sin_h).astype(bf16)
            s_ref[part, :] = (cos_h * sin_h).astype(bf16)
        return carry

    lax.fori_loop(0, a_ref.shape[0] // rb, body, 0)


def far_table(a, b):
    rows = a.shape[0]
    recv = b.shape[1]
    tb = chunk_of(recv, 256)
    rb = chunk_of(rows, 1024)
    col = lambda n: pl.BlockSpec((n, tb), lambda i: (0, i))
    out = jax.ShapeDtypeStruct((rows, recv), bf16)
    cells = rows * recv
    return pl.pallas_call(
        lambda *refs: table_body(rb, *refs),
        grid=(recv // tb,),
        in_specs=[pl.BlockSpec(a.shape, lambda i: (0, 0)), col(32)],
        out_specs=[col(rows), col(rows)],
        out_shape=[out, out],
        compiler_params=pltpu.CompilerParams(vmem_limit_bytes=48 * 2**20),
        cost_estimate=pl.CostEstimate(flops=cells * 30, bytes_accessed=4 * cells, transcendentals=0),
        name="far_table",
    )(a, b)


def on_device(panel_angles, impedance, quad_count, receivers, farfield_data, warm_density):
    rows = impedance.shape[0]
    count_dir = farfield_data.shape[1]
    groups = lax.axis_size("dir")
    blocks = lax.axis_size("elem")
    ndir = count_dir * groups
    sub = rows // groups
    me = lax.axis_index("dir")

    w_loc = weights(quad_count)
    wz_loc = w_loc * impedance
    pos_loc = positions(panel_angles)
    turn_loc = pos_loc * TURNS

    src = lax.dynamic_slice_in_dim(turn_loc, me * sub, sub, 1)
    v = (wz_loc * warm_density).astype(bf16)
    v = jnp.transpose(v.reshape(2 * count_dir, groups, sub), (1, 0, 2))

    left, right = distance_rows(src, turn_loc)
    tb = chunk_of(rows, 256)
    right = jnp.transpose(right.reshape(right.shape[0], rows // tb, tb), (1, 0, 2))
    cos_k, sin_k, v_all, image = forward(left, right, v, blocks)
    image = image.reshape(2, count_dir, rows)

    dvec = lattice(me * count_dir + jnp.arange(count_dir, dtype=jnp.int32), ndir)
    state = plane(dvec, pos_loc) - image

    left, right = product_rows(turn_loc, lattice(receivers, RBANK))
    cos_t, sin_t = far_table(pad_rows(left).T, pad_rows(right))
    pair = 2 * count_dir
    recv = farfield_data.shape[2]
    data = jnp.transpose(farfield_data.reshape(pair, blocks, recv // blocks), (1, 0, 2))
    moved = (w_loc * state).astype(bf16).reshape(pair, rows)
    grad = backward(moved, data, w_loc[None], cos_t, sin_t, cos_k, sin_k, v_all)
    return (grad[:, 0].reshape(rows) / (-ndir * wz_loc), state)


def solution(mesh):
    placed = (
        P(None, "elem"),
        P("elem"),
        P("elem"),
        P(),
        P(None, "dir", None),
        P(None, "dir", "elem"),
    )
    return jax.shard_map(
        on_device,
        mesh=mesh,
        in_specs=placed,
        out_specs=(P("elem"), P(None, "dir", "elem")),
        check_vma=False,
    )
```
